128 devices in a mesh: shard: 16 (over x, z_hi, core), tensor: 8 (over z_lo, y).
Axes of the slice: x: 4, y: 4, z: 4 (z_hi: 2, z_lo: 2; z = z_hi * 2 + z_lo), core: 2. Of those that a mesh axis runs over, the one named last changes fastest.
Arguments:
- hidden_in: bfloat16 [12288, 8192], P('shard'), may hold values from -720 to 720
- policy_weights: bfloat16 [2, 8192, 1024], P(None, 'shard', 'tensor'), may hold values from -6 to 6
- reference_weights: bfloat16 [2, 8192, 1024], P(None, None, 'tensor'), may hold values from -6 to 6
- policy_queries: bfloat16 [12288, 4096], P('shard', 'tensor'), may hold values from -180 to 180
- reference_queries: bfloat16 [12288, 4096], P('shard', 'tensor'), may hold values from -180 to 180
- readout: bfloat16 [12288, 4096], P('shard', 'tensor'), may hold values from -90 to 90
- lengths: int32 [32], P('shard'), may hold values from 96 to 384, as said below
Outputs:
- new_policy: bfloat16 [2, 8192, 1024], P(None, 'shard', 'tensor')
- new_reference: bfloat16 [2, 8192, 1024], P(None, None, 'tensor')
- margins: float32 [16], P('shard')
The draws below stay inside these ranges and needn't reach their ends.
Inputs may be any that keep to these rules, and one draw needn't show every extreme that they name: The first lengths[s] positions of sequence s are real, the rest padding; some sequence has all 384 real.
All inputs are finite; a program needn't handle non-finite values.
Results may differ from the reference program's by a relative error of at most 0.0087.
Values may be sent and summed in bfloat16 or wider, within the bound.
A program may use at most 128 MiB of HBM per device.

```python
import math
import jax
import jax.numpy as jnp
from jax import lax

D = 8192
HD = 128
KVH = 8
QH = 32
LEN = 384
SEQS = 32
TOKENS = 12288
N_SHARD = 16


def draw_hidden_in(key, part):
    key = jax.random.fold_in(key, 11)
    first_key, second_key = jax.random.split(key, 2)
    feature_rank = jnp.arange(D).astype(jnp.float32) / D
    column_scale = 10.0 ** jax.random.uniform(first_key, (D,)) * 3.0 ** (0.5 * feature_rank)
    base_values = jnp.clip(jax.random.normal(second_key, (TOKENS, D)), -5.0, 5.0)
    return (base_values * column_scale).astype(jnp.bfloat16)


def draw_policy_queries(key, part):
    key = jax.random.fold_in(key, 21)
    first_key = jax.random.fold_in(key, 0)
    row_width = QH * HD
    return jnp.clip(jax.random.normal(first_key, (TOKENS, row_width)), -5.0, 5.0).astype(jnp.bfloat16)


def draw_reference_queries(key, part):
    key = jax.random.fold_in(key, 27)
    first_key = jax.random.fold_in(key, 0)
    row_width = QH * HD
    return jnp.clip(jax.random.normal(first_key, (TOKENS, row_width)), -5.0, 5.0).astype(jnp.bfloat16)


def draw_readout(key, part):
    key = jax.random.fold_in(key, 31)
    first_key, second_key = jax.random.split(key, 2)
    row_width = QH * HD
    head_rank = (jnp.arange(row_width) // HD).astype(jnp.float32) / QH
    column_scale = 10.0 ** jax.random.uniform(first_key, (row_width,)) * 3.0 ** (0.5 * head_rank)
    base_values = jnp.clip(jax.random.normal(second_key, (TOKENS, row_width)), -5.0, 5.0)
    return (base_values * column_scale).astype(jnp.bfloat16)


def draw_lengths(key, part):
    key = jax.random.fold_in(key, 41)
    first_key, second_key = jax.random.split(key)
    drawn_lengths = jax.random.randint(first_key, (SEQS,), LEN // 4, LEN + 1)
    longest = jax.random.randint(second_key, (), 0, SEQS)
    return drawn_lengths.at[longest].set(LEN).astype(jnp.int32)


def block_scale(key, extent, cuts, low, top_value):
    gain = 1.0
    for axis_at, blocks in cuts:
        steps = jax.random.uniform(jax.random.fold_in(jax.random.fold_in(key, 6), axis_at), (blocks,), jnp.float32, low / len(cuts), top_value / len(cuts))
        gain = gain * jnp.repeat(jnp.exp(steps), extent[axis_at] // blocks).reshape((-1,) + (1,) * (len(extent) - 1 - axis_at))
    return gain


def centred(stream_key, extent, spread, most, shards=(), kind=jnp.bfloat16):
    drawn = spread * jax.random.normal(stream_key, extent, jnp.float32)
    if shards:
        drawn = drawn * block_scale(stream_key, extent, shards, -0.22, 0.18)
    return jnp.clip(drawn, -most, most).astype(kind)


def setup_inputs(seed: int = 0) -> dict:
    key_list = jax.random.split(jax.random.key(seed), 8)
    hidden_in = draw_hidden_in(jax.random.fold_in(key_list[7], 71), 0)
    policy_weights = centred(key_list[1], (2, D, KVH * HD), 1.0, 6.0, ((1, 16), (2, 8)))
    reference_weights = centred(key_list[2], (2, D, KVH * HD), 1.0, 6.0, ((2, 8),))
    policy_queries = draw_policy_queries(jax.random.fold_in(key_list[7], 71), 0)
    reference_queries = draw_reference_queries(jax.random.fold_in(key_list[7], 71), 0)
    readout = draw_readout(jax.random.fold_in(key_list[7], 71), 0)
    lengths = draw_lengths(jax.random.fold_in(key_list[7], 71), 0)
    return dict(hidden_in=hidden_in, policy_weights=policy_weights, reference_weights=reference_weights, policy_queries=policy_queries, reference_queries=reference_queries, readout=readout, lengths=lengths)


rope_base = 1000000.0
dpo_beta = 0.1
learning_rate = 0.2
mix_alpha = 0.6
norm_eps = 1e-06

def rope_tables(seq_count, seq_len, head_size):
    positions = jnp.tile(jnp.arange(seq_len, dtype=jnp.float32), seq_count)
    freq_index = jnp.arange(head_size // 2, dtype=jnp.float32)
    frequency = rope_base ** (-2.0 * freq_index / head_size)
    angles = positions[:, None] * frequency[None, :]
    return (jnp.cos(angles)[:, None, :], jnp.sin(angles)[:, None, :])

def rotate_half(vectors, cosine, sine_table):
    half_size = vectors.shape[-1] // 2
    first_half = vectors[..., :half_size]
    second_half = vectors[..., half_size:]
    return jnp.concatenate([first_half * cosine - second_half * sine_table, second_half * cosine + first_half * sine_table], axis=-1)

def rounded(values):
    return lax.optimization_barrier(values.astype(jnp.bfloat16)).astype(jnp.float32)

def masked_scores(key_rows, value_rows, queries, readout, lengths, seq_len, total_heads):
    seq_count = lengths.shape[0]
    kv_heads = key_rows.shape[1]
    head_size = key_rows.shape[2]
    groups = queries.shape[1] // (kv_heads * head_size)
    query_f = queries.reshape(seq_count, seq_len, kv_heads, groups, head_size).astype(jnp.float32)
    key_f = key_rows.reshape(seq_count, seq_len, kv_heads, head_size).astype(jnp.float32)
    value_f = value_rows.reshape(seq_count, seq_len, kv_heads, head_size).astype(jnp.float32)
    logits = jnp.einsum('sikgd,sjkd->skgij', query_f, key_f) / math.sqrt(head_size)
    positions = jnp.arange(seq_len)
    causal = positions[:, None] >= positions[None, :]
    live_keys = positions[None, :] < lengths[:, None]
    allowed = causal[None, None, None, :, :] & live_keys[:, None, None, None, :]
    logits = jnp.where(allowed, logits, -1e+30)
    row_max = lax.optimization_barrier(jnp.max(logits, axis=-1, keepdims=True))
    exponent = jnp.exp(logits - row_max)
    probability = rounded(exponent / lax.optimization_barrier(jnp.sum(exponent, axis=-1, keepdims=True)))
    attended = rounded(jnp.einsum('skgij,sjkd->sikgd', probability, value_f))
    readout_f = readout.reshape(seq_count, seq_len, kv_heads, groups, head_size).astype(jnp.float32)
    token_logit = lax.optimization_barrier(jnp.sum(attended * readout_f, axis=(2, 3, 4))) / math.sqrt(total_heads * head_size)
    return lax.optimization_barrier(jnp.sum(jnp.where(live_keys, token_logit, 0.0), axis=1))

def reference(hidden_in, policy_weights, reference_weights, policy_queries, reference_queries, readout, lengths):
    hidden_f = hidden_in.astype(jnp.float32)
    inverse = lax.rsqrt(lax.optimization_barrier(jnp.mean(hidden_f * hidden_f, axis=-1, keepdims=True)) + norm_eps)
    normed = (hidden_f * inverse).astype(jnp.bfloat16)
    block_rows = 2 * LEN
    columns = KVH * HD
    cosine, sine_table = rope_tables(2, LEN, HD)
    width_scale = D ** (-0.5)
    policy_f = policy_weights.astype(jnp.float32)
    reference_f = reference_weights.astype(jnp.float32)

    def project(rows_in, weights_f):
        projected = jnp.einsum('td,kdc->tkc', rows_in.astype(jnp.float32), weights_f) * width_scale
        key_rows = rotate_half(projected[:, 0].reshape(block_rows, KVH, HD), cosine, sine_table).astype(jnp.bfloat16)
        value_rows = projected[:, 1].reshape(block_rows, KVH, HD).astype(jnp.bfloat16)
        return (key_rows, value_rows)

    def block_slice(array, block_index, row_count):
        return lax.dynamic_slice_in_dim(array, block_index * row_count, row_count, 0)

    def block_scores(block_index):
        rows_in = block_slice(normed, block_index, block_rows)
        seq_lengths = block_slice(lengths, block_index, 2)
        readout_rows = block_slice(readout, block_index, block_rows)
        ref_keys, ref_values = project(rows_in, reference_f)
        pol_keys, pol_values = project(rows_in, policy_f)
        ref_scores = masked_scores(ref_keys, ref_values, block_slice(reference_queries, block_index, block_rows), readout_rows, seq_lengths, LEN, QH)
        pol_scores = masked_scores(pol_keys, pol_values, block_slice(policy_queries, block_index, block_rows), readout_rows, seq_lengths, LEN, QH)
        return (ref_scores, pol_scores)
    blocks = jnp.arange(N_SHARD, dtype=jnp.int32)
    ref_all, pol_all = lax.map(block_scores, blocks)
    paired = pol_all - ref_all
    margins = dpo_beta * (paired[:, 0] - paired[:, 1])
    weight = jax.nn.sigmoid(-margins)
    coefficient = jnp.stack([-weight, weight], axis=1)

    def add_block(running, block_index):
        rows_in = block_slice(normed, block_index, block_rows)
        seq_lengths = block_slice(lengths, block_index, 2)
        readout_rows = block_slice(readout, block_index, block_rows)
        query_rows = block_slice(policy_queries, block_index, block_rows)
        pol_keys, pol_values = project(rows_in, policy_f)

        def policy_part(key_rows, value_rows):
            return masked_scores(key_rows, value_rows, query_rows, readout_rows, seq_lengths, LEN, QH)
        unused_scores, pullback = jax.vjp(policy_part, pol_keys, pol_values)
        block_coeff = lax.dynamic_index_in_dim(coefficient, block_index, 0, keepdims=False)
        key_grad, value_grad = pullback(block_coeff)
        key_pre = rotate_half(key_grad.astype(jnp.float32), cosine, -sine_table).astype(jnp.bfloat16)
        cotangent = jnp.concatenate([key_pre.reshape(block_rows, columns), value_grad.reshape(block_rows, columns)], axis=1)
        row_term = jnp.dot(rows_in.T, cotangent, preferred_element_type=jnp.float32)
        return (running + rounded(row_term), None)
    gradient_sum, unused_out = lax.scan(add_block, jnp.zeros((D, 2 * columns), jnp.float32), blocks)
    gradient = gradient_sum.reshape(D, 2, columns).transpose(1, 0, 2)
    mean_square = lax.optimization_barrier(jnp.mean(gradient * gradient, axis=(1, 2)))
    scale_factor = lax.rsqrt(mean_square + norm_eps)
    new_policy = (policy_f - learning_rate * scale_factor[:, None, None] * gradient).astype(jnp.bfloat16)
    new_reference = (mix_alpha * new_policy.astype(jnp.float32) + (1.0 - mix_alpha) * reference_f).astype(jnp.bfloat16)
    return (new_policy, new_reference, margins)
```

```python
import math

import jax
import jax.numpy as jnp
import numpy as np
from jax import lax
from jax.experimental import pallas as pl
from jax.experimental.pallas import tpu as pltpu
from jax.sharding import PartitionSpec as P

D = 8192
HD = 128
KVH = 8
QH = 32
LEN = 384
TOK = 2 * LEN
HEADS = 4
NS = 16
NT = 8
ROWS = D // NS
QB = 128
NB = LEN // QB

rope_base = 1000000.0
dpo_beta = 0.1
learning_rate = 0.2
mix_alpha = 0.6
norm_eps = 1e-06

MESH = pl.DeviceIdType.MESH
BF = jnp.bfloat16
F32 = jnp.float32

OWN, LFT, RGT, ZED, OPP, ZLF, ZRG, ZOP = range(8)


def rope_constants():
    positions = np.arange(LEN, dtype=np.float32)
    index = np.arange(HD // 2, dtype=np.float32)
    frequency = (np.float32(rope_base) ** (np.float32(-2.0) * index / np.float32(HD))).astype(np.float32)
    angles = (positions[:, None] * frequency[None, :]).astype(np.float32)
    cosine, sine = np.cos(angles), np.sin(angles)
    wide_cos = np.concatenate([cosine, cosine], axis=1)
    wide_sin = np.concatenate([-sine, sine], axis=1)
    return np.stack([wide_cos, wide_sin]), np.stack([wide_cos.T[: HD // 2], sine.T])


def dot(a, b, contract=((1,), (0,))):
    return lax.dot_general(a, b, (contract, ((), ())), preferred_element_type=F32)


def kernel(
    hid, pw, rw, pq, rq, ro, lens, rope, rope_t,
    newp, newr, marg,
    normed, pfull, gfull, rwv, pqv, rqv, rov, ropev, ropetv,
    acc, keys, values, cot, probs, grad_t,
    partial, sib_send, sib_recv, stage, net_recv,
    score_buf, sq_tensor, sq_shard, newp_v,
    hid_sem, load_sem, store_sem,
    g1_send, g1_recv, s1_send, s1_recv,
    g2_send, g2_recv, s2_send, s2_recv,
    rs_sib_send, rs_sib_recv, rs_send, rs_recv,
    sc_send, sc_recv, qt_send, qt_recv, qs_send, qs_recv,
):
    s = lax.axis_index("shard")
    t = lax.axis_index("tensor")
    x, h, c = s // 4, (s // 2) % 2, s % 2

    def shard_of(xx, hh, cc):
        return lax.rem(xx, 4) * 4 + hh * 2 + cc

    left = (shard_of(x + 3, h, c), t)
    right = (shard_of(x + 1, h, c), t)
    zed = (shard_of(x, 1 - h, c), t)
    sib = (shard_of(x, h, 1 - c), t)

    pair = {
        OWN: (x, h),
        LFT: (x + 3, h),
        RGT: (x + 1, h),
        ZED: (x, 1 - h),
        OPP: (x + 2, h),
        ZLF: (x + 3, 1 - h),
        ZRG: (x + 1, 1 - h),
        ZOP: (x + 2, 1 - h),
    }

    def rows_of(pos, cc):
        return pl.ds(pl.multiple_of(shard_of(*pair[pos], cc) * ROWS, ROWS), ROWS)

    def pair_rows(pos):
        return pl.ds(pl.multiple_of(shard_of(*pair[pos], 0) * ROWS, 2 * ROWS), 2 * ROWS)

    pending = []

    def send(src, dst, send_sem, recv_sem, device):
        copy = pltpu.make_async_remote_copy(
            src_ref=src, dst_ref=dst, send_sem=send_sem, recv_sem=recv_sem,
            device_id=device, device_id_type=MESH,
        )
        copy.start()
        pending.append(copy)

    def arrived(dst, recv_sem, send_sem, device):
        pltpu.make_async_remote_copy(
            src_ref=dst, dst_ref=dst, send_sem=send_sem, recv_sem=recv_sem,
            device_id=device, device_id_type=MESH,
        ).wait_recv()

    loads = []

    def load(src, dst, i):
        copy = pltpu.make_async_copy(src, dst, load_sem.at[i])
        copy.start()
        loads.append(copy)

    hid_copies = []
    for b in range(3):
        copy = pltpu.make_async_copy(hid.at[pl.ds(256 * b, 256)], normed.at[pl.ds(256 * b, 256)], hid_sem.at[b])
        copy.start()
        hid_copies.append(copy)
        if b == 0:
            load(rw, rwv, 0)
    load(rq, rqv, 1)
    load(ro, rov, 2)
    load(rope, ropev, 3)
    load(pq, pqv, 4)
    load(rope_t, ropetv, 5)
    own_rows = rows_of(OWN, c)
    load(pw, pfull.at[:, own_rows, :], 6)

    barrier = pltpu.get_barrier_semaphore()
    for r in range(1, NS):
        pl.semaphore_signal(barrier, inc=1, device_id=(lax.rem(s + r, NS), t), device_id_type=MESH)
    for r in range(1, NT):
        pl.semaphore_signal(barrier, inc=1, device_id=(s, lax.rem(t + r, NT)), device_id_type=MESH)
    pl.semaphore_wait(barrier, NS + NT - 2)

    class Gather:
        def __init__(self, buf, own, send_sem, recv_sem, sib_send_sem, sib_recv_sem):
            self.buf, self.own = buf, own
            self.send_sem, self.recv_sem = send_sem, recv_sem
            self.sib_send_sem, self.sib_recv_sem = sib_send_sem, sib_recv_sem
            self.count = 0

        def block(self, pos, cc, k):
            return self.buf.at[k, rows_of(pos, cc), :]

        def to(self, src, dst_pos_here, k, arrive_as, device):
            send(src, self.block(dst_pos_here, c, k), self.send_sem.at[self.count],
                 self.recv_sem.at[arrive_as, k], device)
            self.count += 1

        def to_sib(self, src, pos, k):
            send(src, self.block(pos, c, k), self.sib_send_sem.at[pos, k], self.sib_recv_sem.at[pos, k], sib)

        def start(self, k):
            src = self.own(k)
            self.to(src, OWN, k, LFT, right)
            self.to(src, OWN, k, RGT, left)
            self.to(src, OWN, k, ZED, zed)
            self.to_sib(src, OWN, k)

        def take(self, pos, k, device):
            arrived(self.block(pos, c, k), self.recv_sem.at[pos, k], self.send_sem.at[0], device)
            src = self.block(pos, c, k)
            if pos == LFT and k == 0:
                self.to(src, pos, k, OPP, right)
            if pos == RGT and k == 1:
                self.to(src, pos, k, OPP, left)
            if pos == ZED:
                self.to(src, pos, k, ZLF, right)
                self.to(src, pos, k, ZRG, left)
            if pos == OPP:
                self.to(src, pos, k, ZOP, zed)
            self.to_sib(src, pos, k)

        def event(self, i):
            if i == 0:
                self.take(LFT, 0, left)
                self.take(RGT, 1, right)
                self.take(ZED, 0, zed)
            elif i == 1:
                self.take(LFT, 1, left)
                self.take(RGT, 0, right)
                self.take(ZED, 1, zed)
            elif i == 2:
                self.take(OPP, 0, left)
                self.take(OPP, 1, right)
            else:
                self.take(ZLF, i - 3, left)
                self.take(ZRG, i - 3, right)
                self.take(ZOP, i - 3, zed)

        def from_sib(self, pos):
            for k in range(2):
                arrived(self.block(pos, 1 - c, k), self.sib_recv_sem.at[pos, k], self.sib_send_sem.at[pos, k], sib)

    g1 = Gather(pfull, lambda k: pw.at[k], g1_send, g1_recv, s1_send, s1_recv)
    g1.start(0)
    g1.start(1)

    def normalise(b):
        hid_copies[b].wait()

        @pl.loop(0, 8)
        def _(i):
            rows = pl.ds(pl.multiple_of(256 * b + i * 32, 32), 32)
            total = jnp.zeros((32, 512), F32)
            for j in range(D // 512):
                part = normed[rows, pl.ds(512 * j, 512)].astype(F32)
                total = total + part * part
            inverse = lax.rsqrt(jnp.sum(total, axis=-1, keepdims=True) * (1.0 / D) + norm_eps)
            for j in range(D // 512):
                cols = pl.ds(512 * j, 512)
                normed[rows, cols] = (normed[rows, cols].astype(F32) * inverse).astype(BF)

    def project(rows, weights, cols, first):
        both = jnp.concatenate([weights[0, cols, :], weights[1, cols, :]], axis=1)
        product = dot(normed[rows, cols], both)
        acc[rows, :] = product if first else acc[rows, :] + product

    def project_reference(b):
        rows = pl.ds(256 * b, 256)
        acc[rows, :] = jnp.zeros((256, 2 * HD), F32)

        @pl.loop(0, 8)
        def _(j):
            project(rows, rwv, pl.ds(pl.multiple_of(j * 1024, 1024), 1024), False)

    def heads_out(which):
        for q in range(2):
            rows = pl.ds(LEN * q, LEN)
            raw = acc[rows, 0:HD] * (D ** -0.5)
            turned = raw * ropev[0] + pltpu.roll(raw, HD // 2, 1) * ropev[1]
            keys[rows, :] = turned.astype(BF)
            values[rows, :] = (acc[rows, HD:] * (D ** -0.5)).astype(BF)

    def stacked(ref, q, b):
        rows = pl.ds(LEN * q + QB * b, QB)
        return jnp.concatenate([ref[rows, pl.ds(HD * g, HD)] for g in range(HEADS)], axis=0)

    def attend(q, b, queries, keep):
        n = QB * (b + 1)
        live = lens[q]
        seen = pl.ds(LEN * q, n)
        logits = dot(stacked(queries, q, b), keys[seen, :], ((1,), (1,))) * (1.0 / math.sqrt(HD))
        row = lax.broadcasted_iota(jnp.int32, (HEADS * QB, n), 0)
        at = QB * b + lax.rem(row, QB)
        key_at = lax.broadcasted_iota(jnp.int32, (HEADS * QB, n), 1)
        allowed = jnp.logical_and(key_at <= at, key_at < live)
        logits = jnp.where(allowed, logits, -1e30)
        exponent = jnp.exp(logits - jnp.max(logits, axis=-1, keepdims=True))
        probability = exponent / jnp.sum(exponent, axis=-1, keepdims=True)
        if keep:
            probs[q, b, :, 0:n] = probability
        attended = dot(probability.astype(BF), values[seen, :]).astype(BF).astype(F32)
        product = attended * stacked(rov, q, b).astype(F32)
        real = QB * b + lax.rem(lax.broadcasted_iota(jnp.int32, product.shape, 0), QB) < live
        product = jnp.where(real, product, 0.0)
        return jnp.sum(product.reshape(HEADS * QB // 8, 8, HD), axis=0)

    def scores(queries, keep):
        chosen = jnp.zeros((8, HD), F32)
        rejected = jnp.zeros((8, HD), F32)
        for b in range(NB):
            chosen = chosen + attend(0, b, queries, keep)
            rejected = rejected + attend(1, b, queries, keep)
        return chosen - rejected

    loads[0].wait()
    for b in range(3):
        normalise(b)
        project_reference(b)
        g1.event(b)
    for i in (1, 2, 3):
        loads[i].wait()
    heads_out(rqv)
    score_buf[t] = -scores(rqv, False)

    everyone = pl.ds(0, TOK)

    def project_policy(pos, first=False):
        g1.from_sib(pos)
        project(everyone, pfull, pair_rows(pos), first)

    loads[6].wait()
    loads[4].wait()
    loads[5].wait()
    project_policy(OWN, True)
    g1.event(3)
    for pos in (LFT, RGT, ZED, OPP):
        project_policy(pos)
    g1.event(4)
    for pos in (ZLF, ZRG, ZOP):
        project_policy(pos)

    heads_out(pqv)
    score_buf[t] = score_buf[t] + scores(pqv, True)
    for r in range(1, NT):
        send(score_buf.at[t], score_buf.at[t], sc_send.at[r], sc_recv.at[t], (s, lax.rem(t + r, NT)))

    def pull(q, b):
        n = QB * (b + 1)
        live = lens[q]
        seen = pl.ds(LEN * q, n)
        sign = -1.0 if q == 0 else 1.0
        out_cot = stacked(rov, q, b).astype(F32) * (sign / math.sqrt(QH * HD))
        real = QB * b + lax.rem(lax.broadcasted_iota(jnp.int32, out_cot.shape, 0), QB) < live
        out_cot = jnp.where(real, out_cot, 0.0).astype(BF)
        probability = probs[q, b, :, 0:n]
        prob_cot = dot(out_cot, values[seen, :], ((1,), (1,))).astype(BF).astype(F32)
        weighted = probability * prob_cot
        logit_cot = weighted - probability * jnp.sum(weighted, axis=-1, keepdims=True)
        value_t = dot(out_cot, probability.astype(BF), ((0,), (0,)))
        key_t = dot(stacked(pqv, q, b), logit_cot.astype(BF), ((0,), (0,)))
        if b == NB - 1:
            grad_t[0, :, seen] = key_t
            grad_t[1, :, seen] = value_t
        else:
            grad_t[0, :, seen] += key_t
            grad_t[1, :, seen] += value_t

    for q in range(2):
        for b in reversed(range(NB)):
            pull(q, b)
        tokens = pl.ds(LEN * q, LEN)
        key_grad = (grad_t[0, :, tokens] * (1.0 / math.sqrt(HD))).astype(BF).astype(F32)
        upper, lower = key_grad[: HD // 2], key_grad[HD // 2 :]
        cosine, sine = ropetv[0], ropetv[1]
        cot[0 : HD // 2, tokens] = (upper * cosine + lower * sine).astype(BF)
        cot[HD // 2 : HD, tokens] = (lower * cosine - upper * sine).astype(BF)
        cot[HD:, tokens] = grad_t[1, :, tokens].astype(BF)

    for r in range(1, NT):
        peer = lax.rem(t + r, NT)
        arrived(score_buf.at[peer], sc_recv.at[peer], sc_send.at[r], (s, peer))
    score_total = score_buf[0]
    for r in range(1, NT):
        score_total = score_total + score_buf[r]
    score_total = jnp.sum(jnp.sum(score_total, axis=1, keepdims=True), axis=0, keepdims=True)
    margin = score_total * (dpo_beta / math.sqrt(QH * HD))
    marg[...] = jnp.broadcast_to(margin, (8, HD))
    weight = 1.0 / (1.0 + jnp.exp(margin))

    def product_of(pos, cc):
        out = dot(cot[...], normed[:, rows_of(pos, cc)]) * weight
        return out[:HD].T, out[HD:].T

    order = (ZOP, ZRG, ZLF, OPP, ZED, RGT, LFT, OWN)
    sends = [0]

    def push(i, k, slot, device):
        send(stage.at[i, k], net_recv.at[slot, k], rs_send.at[sends[0]], rs_recv.at[slot, k], device)
        sends[0] += 1

    def pull_net(slot, k, device):
        arrived(net_recv.at[slot, k], rs_recv.at[slot, k], rs_send.at[0], device)
        return net_recv[slot, k].astype(F32)

    SLOT_Z1, SLOT_R2L, SLOT_R2R, SLOT_3, SLOT_Z4, SLOT_5L, SLOT_5R = range(7)

    def compute(i):
        for k, block in enumerate(product_of(order[i], 1 - c)):
            sib_send[i, k] = block.astype(BF)
        send(sib_send.at[i], sib_recv.at[i], rs_sib_send.at[i], rs_sib_recv.at[i], sib)
        for k, block in enumerate(product_of(order[i], c)):
            partial[i, k] = block

    def settle(i):
        arrived(sib_recv.at[i], rs_sib_recv.at[i], rs_sib_send.at[i], sib)

    def put(i, k, terms):
        total = partial[i, k] + sib_recv[i, k].astype(F32)
        for term in terms:
            total = total + term
        stage[i, k] = total.astype(BF)

    compute(0)
    compute(1)
    settle(0)
    for k in range(2):
        put(0, k, ())
        push(0, k, SLOT_Z1, zed)
    compute(2)
    settle(1)
    for k in range(2):
        put(1, k, ())
        push(1, k, SLOT_R2L, right)
    compute(3)
    settle(2)
    for k in range(2):
        put(2, k, ())
        push(2, k, SLOT_R2R, left)
    for i in range(4, 8):
        compute(i)
    for i in range(3, 8):
        settle(i)
    put(3, 0, (pull_net(SLOT_Z1, 0, zed),))
    push(3, 0, SLOT_3, right)
    put(3, 1, (pull_net(SLOT_Z1, 1, zed),))
    push(3, 1, SLOT_3, left)
    put(5, 1, ())
    push(5, 1, SLOT_5L, right)
    put(6, 0, ())
    push(6, 0, SLOT_5R, left)
    for k in range(2):
        put(4, k, (pull_net(SLOT_R2L, k, left), pull_net(SLOT_R2R, k, right)))
        push(4, k, SLOT_Z4, zed)
    put(5, 0, (pull_net(SLOT_3, 0, left),))
    push(5, 0, SLOT_5L, right)
    put(6, 1, (pull_net(SLOT_3, 1, right),))
    push(6, 1, SLOT_5R, left)

    g2 = Gather(gfull, lambda k: gfull.at[k, own_rows, :], g2_send, g2_recv, s2_send, s2_recv)
    for k in range(2):
        total = partial[7, k] + sib_recv[7, k].astype(F32)
        total = total + pull_net(SLOT_Z4, k, zed)
        total = total + pull_net(SLOT_5L, k, left)
        total = total + pull_net(SLOT_5R, k, right)
        gfull[k, own_rows, :] = total.astype(BF)
        g2.start(k)
        sq_tensor[t, k] = jnp.sum((total * total).reshape(ROWS // 8, 8, HD), axis=0)

    for r in range(1, NT):
        send(sq_tensor.at[t], sq_tensor.at[t], qt_send.at[r], qt_recv.at[t], (s, lax.rem(t + r, NT)))
    for r in range(1, NT):
        peer = lax.rem(t + r, NT)
        arrived(sq_tensor.at[peer], qt_recv.at[peer], qt_send.at[r], (s, peer))
    squares = sq_tensor[0]
    for r in range(1, NT):
        squares = squares + sq_tensor[r]
    sq_shard[s] = squares
    for r in range(1, NS):
        send(sq_shard.at[s], sq_shard.at[s], qs_send.at[r], qs_recv.at[s], (lax.rem(s + r, NS), t))
    g2.event(0)
    for r in range(1, NS):
        peer = lax.rem(s + r, NS)
        arrived(sq_shard.at[peer], qs_recv.at[peer], qs_send.at[r], (peer, t))
    squares = sq_shard[0]
    for r in range(1, NS):
        squares = squares + sq_shard[r]
    step = []
    for k in range(2):
        mean = jnp.sum(jnp.sum(squares[k], axis=1, keepdims=True), axis=0, keepdims=True) * (1.0 / (D * KVH * HD))
        step.append(learning_rate * lax.rsqrt(mean + norm_eps))

    stores = []

    def store(src, dst, i):
        copy = pltpu.make_async_copy(src, dst, store_sem.at[i])
        copy.start()
        stores.append(copy)

    def update(pos):
        g2.from_sib(pos)
        base = shard_of(*pair[pos], 0) * ROWS
        for k in range(2):

            @pl.loop(0, 8)
            def _(i):
                rows = pl.ds(pl.multiple_of(base + i * 128, 128), 128)
                fresh = (pfull[k, rows, :].astype(F32) - step[k] * gfull[k, rows, :].astype(F32)).astype(BF)
                if pos == OWN:
                    newp_v[k, pl.ds(pl.multiple_of(i * 128, 128), 128), :] = fresh
                mixed = mix_alpha * fresh.astype(F32) + (1.0 - mix_alpha) * rwv[k, rows, :].astype(F32)
                rwv[k, rows, :] = mixed.astype(BF)

            store(rwv.at[k, pair_rows(pos), :], newr.at[k, pair_rows(pos), :], 2 * pos + k)
        if pos == OWN:
            store(newp_v.at[:, pl.ds(pl.multiple_of(c * ROWS, ROWS), ROWS), :], newp, 16)

    g2.event(1)
    update(OWN)
    g2.event(2)
    for pos in (LFT, RGT, ZED):
        update(pos)
    g2.event(3)
    update(OPP)
    g2.event(4)
    for pos in (ZLF, ZRG, ZOP):
        update(pos)
    for copy in stores:
        copy.wait()
    for copy in pending:
        copy.wait_send()


def body(hidden_in, policy_weights, reference_weights, policy_queries, reference_queries, readout, lengths):
    rope, rope_t = rope_constants()
    anywhere = pl.BlockSpec(memory_space=pl.ANY)
    dma = pltpu.SemaphoreType.DMA
    block = (2, ROWS, HD)
    new_rows, new_reference, margins = pl.pallas_call(
        kernel,
        out_shape=(
            jax.ShapeDtypeStruct(block, BF),
            jax.ShapeDtypeStruct((2, D, HD), BF),
            jax.ShapeDtypeStruct((8, HD), F32),
        ),
        in_specs=[anywhere] * 6 + [pl.BlockSpec(memory_space=pltpu.SMEM)] + [anywhere] * 2,
        out_specs=(anywhere, anywhere, pl.BlockSpec(memory_space=pltpu.VMEM)),
        scratch_shapes=[
            pltpu.VMEM((TOK, D), BF),
            pltpu.VMEM((2, D, HD), BF),
            pltpu.VMEM((2, D, HD), BF),
            pltpu.VMEM((2, D, HD), BF),
            pltpu.VMEM((TOK, HEADS * HD), BF),
            pltpu.VMEM((TOK, HEADS * HD), BF),
            pltpu.VMEM((TOK, HEADS * HD), BF),
            pltpu.VMEM((2, LEN, HD), F32),
            pltpu.VMEM((2, HD // 2, LEN), F32),
            pltpu.VMEM((TOK, 2 * HD), F32),
            pltpu.VMEM((TOK, HD), BF),
            pltpu.VMEM((TOK, HD), BF),
            pltpu.VMEM((2 * HD, TOK), BF),
            pltpu.VMEM((2, NB, HEADS * QB, LEN), F32),
            pltpu.VMEM((2, HD, TOK), F32),
            pltpu.VMEM((8, *block), F32),
            pltpu.VMEM((8, *block), BF),
            pltpu.VMEM((8, *block), BF),
            pltpu.VMEM((8, *block), BF),
            pltpu.VMEM((7, *block), BF),
            pltpu.VMEM((NT, 8, HD), F32),
            pltpu.VMEM((NT, 2, 8, HD), F32),
            pltpu.VMEM((NS, 2, 8, HD), F32),
            pltpu.VMEM((2, 2 * ROWS, HD), BF),
            dma((3,)), dma((7,)), dma((17,)),
            dma((14,)), dma((8, 2)), dma((8, 2)), dma((8, 2)),
            dma((14,)), dma((8, 2)), dma((8, 2)), dma((8, 2)),
            dma((8,)), dma((8,)), dma((14,)), dma((7, 2)),
            dma((NT,)), dma((NT,)), dma((NT,)), dma((NT,)), dma((NS,)), dma((NS,)),
        ],
        compiler_params=pltpu.CompilerParams(
            collective_id=0, has_side_effects=True, vmem_limit_bytes=60 * 1024 * 1024
        ),
        cost_estimate=pl.CostEstimate(flops=12_000_000_000, bytes_accessed=24_000_000, transcendentals=2_000_000),
    )(
        hidden_in, policy_weights, reference_weights, policy_queries, reference_queries, readout, lengths,
        jnp.asarray(rope), jnp.asarray(rope_t),
    )
    return new_rows, new_reference, margins[0, :1]


def solution(mesh):
    return jax.shard_map(
        body,
        mesh=mesh,
        in_specs=(
            P("shard", None),
            P(None, "shard", "tensor"),
            P(None, None, "tensor"),
            P("shard", "tensor"),
            P("shard", "tensor"),
            P("shard", "tensor"),
            P("shard"),
        ),
        out_specs=(P(None, "shard", "tensor"), P(None, None, "tensor"), P("shard")),
        check_vma=False,
    )
```

```python
import math

import jax
import jax.numpy as jnp
import numpy as np
from jax import lax
from jax.experimental import pallas as pl
from jax.experimental.pallas import tpu as pltpu
from jax.sharding import PartitionSpec as P

D = 8192
HD = 128
KVH = 8
QH = 32
LEN = 384
TOK = 2 * LEN
HEADS = 4
NS = 16
NT = 8
ROWS = D // NS
QB = 128
NB = LEN // QB

rope_base = 1000000.0
dpo_beta = 0.1
learning_rate = 0.2
mix_alpha = 0.6
norm_eps = 1e-06

MESH = pl.DeviceIdType.MESH
BF = jnp.bfloat16
F32 = jnp.float32

OWN, LFT, RGT, ZED, OPP, ZLF, ZRG, ZOP = range(8)


def rope_constants():
    positions = np.arange(LEN, dtype=np.float32)
    index = np.arange(HD // 2, dtype=np.float32)
    frequency = (np.float32(rope_base) ** (np.float32(-2.0) * index / np.float32(HD))).astype(np.float32)
    angles = (positions[:, None] * frequency[None, :]).astype(np.float32)
    cosine, sine = np.cos(angles), np.sin(angles)
    wide_cos = np.concatenate([cosine, cosine], axis=1)
    wide_sin = np.concatenate([-sine, sine], axis=1)
    return np.stack([wide_cos, wide_sin]), np.stack([wide_cos.T[: HD // 2], sine.T])


def dot(a, b, contract=((1,), (0,))):
    return lax.dot_general(a, b, (contract, ((), ())), preferred_element_type=F32)


def kernel(
    hid, pw, rw, pq, rq, ro, lens, rope, rope_t,
    newp, newr, marg,
    normed, pfull, gfull, rwv, pqv, rqv, rov, ropev, ropetv,
    acc, keys, values, cot, probs, grad_t,
    partial, sib_send, sib_recv, stage, net_recv,
    score_buf, sq_tensor, sq_shard,
    hid_sem, load_sem,
    g1_send, g1_recv, s1_send, s1_recv,
    g2_send, g2_recv, s2_send, s2_recv,
    rs_sib_send, rs_sib_recv, rs_send, rs_recv,
    sc_send, sc_recv, qt_send, qt_recv, qs_send, qs_recv,
):
    s = lax.axis_index("shard")
    t = lax.axis_index("tensor")
    x, h, c = s // 4, (s // 2) % 2, s % 2

    def shard_of(xx, hh, cc):
        return lax.rem(xx, 4) * 4 + hh * 2 + cc

    left = (shard_of(x + 3, h, c), t)
    right = (shard_of(x + 1, h, c), t)
    zed = (shard_of(x, 1 - h, c), t)
    sib = (shard_of(x, h, 1 - c), t)

    pair = {
        OWN: (x, h),
        LFT: (x + 3, h),
        RGT: (x + 1, h),
        ZED: (x, 1 - h),
        OPP: (x + 2, h),
        ZLF: (x + 3, 1 - h),
        ZRG: (x + 1, 1 - h),
        ZOP: (x + 2, 1 - h),
    }

    def rows_of(pos, cc):
        return pl.ds(pl.multiple_of(shard_of(*pair[pos], cc) * ROWS, ROWS), ROWS)

    def pair_rows(pos):
        return pl.ds(pl.multiple_of(shard_of(*pair[pos], 0) * ROWS, 2 * ROWS), 2 * ROWS)

    def send(src, dst, send_sem, recv_sem, device):
        pltpu.make_async_remote_copy(
            src_ref=src, dst_ref=dst, send_sem=send_sem, recv_sem=recv_sem,
            device_id=device, device_id_type=MESH,
        ).start()

    def all_sent(amount, send_sem, recv_sem):
        pltpu.make_async_remote_copy(
            src_ref=amount, dst_ref=amount, send_sem=send_sem, recv_sem=recv_sem,
            device_id=sib, device_id_type=MESH,
        ).wait_send()

    def arrived(dst, recv_sem, send_sem, device):
        pltpu.make_async_remote_copy(
            src_ref=dst, dst_ref=dst, send_sem=send_sem, recv_sem=recv_sem,
            device_id=device, device_id_type=MESH,
        ).wait_recv()

    barrier = pltpu.get_barrier_semaphore()
    for device in (left, right, zed, sib):
        pl.semaphore_signal(barrier, inc=1, device_id=device, device_id_type=MESH)
    for r in range(1, NT):
        pl.semaphore_signal(barrier, inc=1, device_id=(s, lax.rem(t + r, NT)), device_id_type=MESH)

    def load_hidden(b):
        copy = pltpu.make_async_copy(hid.at[pl.ds(256 * b, 256)], normed.at[pl.ds(256 * b, 256)], hid_sem.at[b])
        copy.start()
        return copy

    def load(src, dst, i):
        copy = pltpu.make_async_copy(src, dst, load_sem.at[i])
        copy.start()
        return copy

    hid_copies = [load_hidden(0)]
    pl.semaphore_wait(barrier, 4 + NT - 1)

    class Gather:
        def __init__(self, buf, own, lead, send_sem, recv_sem, sib_send_sem, sib_recv_sem):
            self.buf, self.own, self.lead = buf, own, lead
            self.send_sem, self.recv_sem = send_sem, recv_sem
            self.sib_send_sem, self.sib_recv_sem = sib_send_sem, sib_recv_sem

        def block(self, pos, cc, k):
            return self.buf.at[k, rows_of(pos, cc), :]

        def to(self, src, dst_pos_here, k, arrive_as, device):
            send(src, self.block(dst_pos_here, c, k), self.send_sem.at[0], self.recv_sem.at[arrive_as, k], device)

        def to_sib(self, src, pos, k):
            send(src, self.block(pos, c, k), self.sib_send_sem.at[0], self.sib_recv_sem.at[pos, k], sib)

        def start(self, k):
            src = self.own(k)
            self.to(src, OWN, k, LFT, right)
            self.to(src, OWN, k, RGT, left)
            self.to(src, OWN, k, ZED, zed)
            self.to_sib(src, OWN, k)

        def start_both(self):
            f, g = self.lead, 1 - self.lead
            self.to(self.own(f), OWN, f, LFT, right)
            self.to(self.own(g), OWN, g, RGT, left)
            self.to(self.own(f), OWN, f, ZED, zed)
            self.to(self.own(g), OWN, g, LFT, right)
            self.to(self.own(f), OWN, f, RGT, left)
            self.to(self.own(g), OWN, g, ZED, zed)
            self.to_sib(self.own(f), OWN, f)
            self.to_sib(self.own(g), OWN, g)

        def take(self, pos, k):
            lead = k == self.lead
            device = {LFT: left, RGT: right, ZED: zed, OPP: left if lead else right, ZLF: left, ZRG: right, ZOP: zed}[pos]
            arrived(self.block(pos, c, k), self.recv_sem.at[pos, k], self.send_sem.at[0], device)
            src = self.block(pos, c, k)
            if pos == LFT and lead:
                self.to(src, pos, k, OPP, right)
            if pos == RGT and not lead:
                self.to(src, pos, k, OPP, left)
            if pos == ZED:
                self.to(src, pos, k, ZLF, right)
                self.to(src, pos, k, ZRG, left)
            if pos == OPP:
                self.to(src, pos, k, ZOP, zed)
            self.to_sib(src, pos, k)

        def from_sib(self, pos, k):
            arrived(self.block(pos, 1 - c, k), self.sib_recv_sem.at[pos, k], self.sib_send_sem.at[0], sib)

        def finish(self):
            all_sent(self.buf.at[:, pl.ds(0, 7 * ROWS), :], self.send_sem.at[0], self.recv_sem.at[LFT, 0])
            all_sent(self.buf.at[:, pl.ds(0, 8 * ROWS), :], self.sib_send_sem.at[0], self.sib_recv_sem.at[OWN, 0])

    g1 = Gather(pfull, lambda k: pw.at[k], 0, g1_send, g1_recv, s1_send, s1_recv)
    g1.start_both()

    hid_copies += [load_hidden(1), load_hidden(2)]
    own_rows = rows_of(OWN, c)
    loads = [
        load(rw, rwv, 0),
        load(rq, rqv, 1),
        load(ro, rov, 2),
        load(rope, ropev, 3),
        load(pw, pfull.at[:, own_rows, :], 4),
        load(pq, pqv, 5),
        load(rope_t, ropetv, 6),
    ]

    def normalise(b):
        hid_copies[b].wait()

        @pl.loop(0, 8)
        def _(i):
            rows = pl.ds(pl.multiple_of(256 * b + i * 32, 32), 32)
            total = jnp.zeros((32, 512), F32)
            for j in range(D // 512):
                part = normed[rows, pl.ds(512 * j, 512)].astype(F32)
                total = total + part * part
            inverse = lax.rsqrt(jnp.sum(total, axis=-1, keepdims=True) * (1.0 / D) + norm_eps)
            for j in range(D // 512):
                cols = pl.ds(512 * j, 512)
                normed[rows, cols] = (normed[rows, cols].astype(F32) * inverse).astype(BF)

    def project(weights, cols, first):
        both = jnp.concatenate([weights[0, cols, :], weights[1, cols, :]], axis=1)
        product = dot(normed[:, cols], both)
        acc[...] = product if first else acc[...] + product

    def project_reference(first, last):
        if first == 0:
            project(rwv, pl.ds(0, 1024), True)
            first = 1

        @pl.loop(first, last)
        def _(j):
            project(rwv, pl.ds(pl.multiple_of(j * 1024, 1024), 1024), False)

    def heads_out():
        for q in range(2):
            rows = pl.ds(LEN * q, LEN)
            raw = acc[rows, 0:HD] * (D ** -0.5)
            turned = raw * ropev[0] + pltpu.roll(raw, HD // 2, 1) * ropev[1]
            keys[rows, :] = turned.astype(BF)
            values[rows, :] = (acc[rows, HD:] * (D ** -0.5)).astype(BF)

    def stacked(ref, q, b):
        rows = pl.ds(LEN * q + QB * b, QB)
        return jnp.concatenate([ref[rows, pl.ds(HD * g, HD)] for g in range(HEADS)], axis=0)

    def attend(q, b, queries, keep):
        n = QB * (b + 1)
        live = lens[q]
        seen = pl.ds(LEN * q, n)
        logits = dot(stacked(queries, q, b), keys[seen, :], ((1,), (1,))) * (math.log2(math.e) / math.sqrt(HD))
        key_at = lax.broadcasted_iota(jnp.int32, (1, n), 1)
        logits = logits + jnp.where(key_at < live, 0.0, -1e30)
        at = lax.broadcasted_iota(jnp.int32, (QB, QB), 0)
        after = lax.broadcasted_iota(jnp.int32, (QB, QB), 1) > at
        corner = jnp.where(after, -1e30, 0.0)
        corner = jnp.concatenate([corner] * HEADS, axis=0)
        if b == 0:
            logits = logits + corner
        else:
            logits = jnp.concatenate([logits[:, : n - QB], logits[:, n - QB :] + corner], axis=1)
        exponent = jnp.exp2(logits - jnp.max(logits, axis=-1, keepdims=True))
        probability = exponent * (1.0 / jnp.sum(exponent, axis=-1, keepdims=True))
        if keep:
            probs[q, b, :, 0:n] = probability
        attended = dot(probability.astype(BF), values[seen, :]).astype(BF).astype(F32)
        product = attended * stacked(rov, q, b).astype(F32)
        real = QB * b + lax.rem(lax.broadcasted_iota(jnp.int32, product.shape, 0), QB) < live
        product = jnp.where(real, product, 0.0)
        return jnp.sum(product.reshape(HEADS * QB // 8, 8, HD), axis=0)

    def scores(queries, keep):
        chosen = jnp.zeros((8, HD), F32)
        rejected = jnp.zeros((8, HD), F32)
        for b in range(NB):
            chosen = chosen + attend(0, b, queries, keep)
            rejected = rejected + attend(1, b, queries, keep)
        return chosen - rejected

    for b in range(3):
        normalise(b)
    for pos, k in ((LFT, 0), (RGT, 1), (ZED, 0)):
        g1.take(pos, k)
    loads[0].wait()
    project_reference(0, 5)
    for pos, k in ((ZED, 1), (LFT, 1), (RGT, 0)):
        g1.take(pos, k)
    project_reference(5, 8)
    for i in (1, 2, 3):
        loads[i].wait()
    heads_out()
    g1.take(OPP, 0)
    g1.take(OPP, 1)
    score_buf[t] = -scores(rqv, False)

    def project_policy(pos, first=False):
        for k in range(2):
            g1.from_sib(pos, k)
        project(pfull, pair_rows(pos), first)

    for i in (4, 5, 6):
        loads[i].wait()
    project_policy(OWN, True)
    g1.take(ZLF, 0)
    g1.take(ZRG, 0)
    for pos in (LFT, RGT, ZED):
        project_policy(pos)
    g1.take(ZOP, 0)
    g1.take(ZLF, 1)
    g1.take(ZRG, 1)
    project_policy(OPP)
    project_policy(ZLF)
    g1.take(ZOP, 1)
    project_policy(ZRG)
    project_policy(ZOP)

    heads_out()
    score_buf[t] = score_buf[t] + scores(pqv, True)
    for r in range(1, NT):
        send(score_buf.at[t], score_buf.at[t], sc_send.at[0], sc_recv.at[0], (s, lax.rem(t + r, NT)))

    def out_cotangent(q, b):
        out_cot = stacked(rov, q, b).astype(F32) * ((-1.0 if q == 0 else 1.0) / math.sqrt(QH * HD))
        real = QB * b + lax.rem(lax.broadcasted_iota(jnp.int32, out_cot.shape, 0), QB) < lens[q]
        return jnp.where(real, out_cot, 0.0).astype(BF)

    def pull_value(q, b):
        n = QB * (b + 1)
        seen = pl.ds(LEN * q, n)
        value_t = dot(out_cotangent(q, b), probs[q, b, :, 0:n].astype(BF), ((0,), (0,)))
        if b == NB - 1:
            grad_t[1, :, seen] = value_t
        else:
            grad_t[1, :, seen] += value_t

    def pull_key(q, b):
        n = QB * (b + 1)
        seen = pl.ds(LEN * q, n)
        probability = probs[q, b, :, 0:n]
        prob_cot = dot(out_cotangent(q, b), values[seen, :], ((1,), (1,))).astype(BF).astype(F32)
        weighted = probability * prob_cot
        logit_cot = weighted - probability * jnp.sum(weighted, axis=-1, keepdims=True)
        key_t = dot(stacked(pqv, q, b), logit_cot.astype(BF), ((0,), (0,)))
        if b == NB - 1:
            grad_t[0, :, seen] = key_t
        else:
            grad_t[0, :, seen] += key_t

    def value_cotangent():
        for q in range(2):
            for b in reversed(range(NB)):
                pull_value(q, b)
        cot[HD:, :] = grad_t[1].astype(BF)

    def key_cotangent(q):
        for b in reversed(range(NB)):
            pull_key(q, b)
        tokens = pl.ds(LEN * q, LEN)
        key_grad = (grad_t[0, :, tokens] * (1.0 / math.sqrt(HD))).astype(BF).astype(F32)
        upper, lower = key_grad[: HD // 2], key_grad[HD // 2 :]
        cosine, sine = ropetv[0], ropetv[1]
        cot[0 : HD // 2, tokens] = (upper * cosine + lower * sine).astype(BF)
        cot[HD // 2 : HD, tokens] = (lower * cosine - upper * sine).astype(BF)

    value_cotangent()
    key_cotangent(0)

    arrived(score_buf.at[pl.ds(0, NT - 1)], sc_recv.at[0], sc_send.at[0], (s, lax.rem(t + 1, NT)))
    score_total = score_buf[0]
    for r in range(1, NT):
        score_total = score_total + score_buf[r]
    score_total = jnp.sum(jnp.sum(score_total, axis=1, keepdims=True), axis=0, keepdims=True)
    margin = score_total * (dpo_beta / math.sqrt(QH * HD))
    marg[...] = jnp.broadcast_to(margin, (8, HD))
    weight = 1.0 / (1.0 + jnp.exp(margin))

    def product_of(pos, cc, k):
        out = dot(cot[pl.ds(HD * k, HD), :], normed[:, rows_of(pos, cc)]) * weight
        return out.T

    order = (ZOP, ZRG, ZLF, OPP, ZED, RGT, LFT, OWN)

    def push(i, k, slot, device):
        send(stage.at[i, k], net_recv.at[slot, k], rs_send.at[0], rs_recv.at[slot, k], device)

    def pull_net(slot, k, device):
        arrived(net_recv.at[slot, k], rs_recv.at[slot, k], rs_send.at[0], device)
        return net_recv[slot, k].astype(F32)

    SLOT_Z1, SLOT_R2L, SLOT_R2R, SLOT_3, SLOT_Z4, SLOT_5L, SLOT_5R = range(7)

    def compute_sib(i, k):
        sib_send[i, k] = product_of(order[i], 1 - c, k).astype(BF)
        send(sib_send.at[i, k], sib_recv.at[i, k], rs_sib_send.at[0], rs_sib_recv.at[i, k], sib)

    def compute_own(i, k):
        partial[i, k] = product_of(order[i], c, k)

    def compute(i, k):
        compute_sib(i, k)
        compute_own(i, k)

    def total_of(i, k, terms):
        arrived(sib_recv.at[i, k], rs_sib_recv.at[i, k], rs_sib_send.at[0], sib)
        total = partial[i, k] + sib_recv[i, k].astype(F32)
        for term in terms:
            total = total + term
        return total

    def put(i, k, slot, device, *terms):
        stage[i, k] = total_of(i, k, terms).astype(BF)
        push(i, k, slot, device)

    f, g = 1, 0
    for i in range(3):
        compute_sib(i, f)
    compute_own(0, f)
    put(0, f, SLOT_Z1, zed)
    compute_own(1, f)
    put(1, f, SLOT_R2L, right)
    compute_own(2, f)
    put(2, f, SLOT_R2R, left)
    key_cotangent(1)
    for i in range(3):
        compute_sib(i, g)
    compute_own(0, g)
    put(0, g, SLOT_Z1, zed)
    compute_own(1, g)
    put(1, g, SLOT_R2L, right)
    compute_own(2, g)
    put(2, g, SLOT_R2R, left)
    compute(3, f)
    compute(6, f)
    put(3, f, SLOT_3, right, pull_net(SLOT_Z1, f, zed))
    compute(4, f)
    put(6, f, SLOT_5R, left)
    compute(3, g)
    put(4, f, SLOT_Z4, zed, pull_net(SLOT_R2L, f, left), pull_net(SLOT_R2R, f, right))
    compute(5, g)
    put(3, g, SLOT_3, left, pull_net(SLOT_Z1, g, zed))
    compute(4, g)
    put(5, g, SLOT_5L, right)
    compute(5, f)
    put(4, g, SLOT_Z4, zed, pull_net(SLOT_R2L, g, left), pull_net(SLOT_R2R, g, right))
    compute(6, g)
    compute(7, f)
    compute(7, g)
    put(5, f, SLOT_5L, right, pull_net(SLOT_3, f, left))
    put(6, g, SLOT_5R, left, pull_net(SLOT_3, g, right))

    g2 = Gather(gfull, lambda k: gfull.at[k, own_rows, :], f, g2_send, g2_recv, s2_send, s2_recv)
    for k in (f, g):
        total = total_of(7, k, (
            pull_net(SLOT_Z4, k, zed), pull_net(SLOT_5L, k, left), pull_net(SLOT_5R, k, right),
        ))
        gfull[k, own_rows, :] = total.astype(BF)
        g2.start(k)
        sq_tensor[t, k] = jnp.sum((total * total).reshape(ROWS // 8, 8, HD), axis=0)

    for r in range(1, NT):
        send(sq_tensor.at[t], sq_tensor.at[t], qt_send.at[0], qt_recv.at[0], (s, lax.rem(t + r, NT)))
    for pos in (LFT, RGT, ZED):
        g2.take(pos, f)
    arrived(sq_tensor.at[pl.ds(0, NT - 1)], qt_recv.at[0], qt_send.at[0], (s, lax.rem(t + 1, NT)))
    squares = sq_tensor[0]
    for r in range(1, NT):
        squares = squares + sq_tensor[r]
    sq_shard[s] = squares
    for r in range(1, NS):
        send(sq_shard.at[s], sq_shard.at[s], qs_send.at[0], qs_recv.at[0], (lax.rem(s + r, NS), t))
    for pos in (ZED, LFT, RGT):
        g2.take(pos, g)
    g2.take(OPP, f)
    g2.take(OPP, g)
    g2.take(ZLF, f)
    g2.take(ZRG, f)
    arrived(sq_shard.at[pl.ds(0, NS - 1)], qs_recv.at[0], qs_send.at[0], (lax.rem(s + 1, NS), t))
    squares = sq_shard[0]
    for r in range(1, NS):
        squares = squares + sq_shard[r]
    step = []
    for k in range(2):
        mean = jnp.sum(jnp.sum(squares[k], axis=1, keepdims=True), axis=0, keepdims=True) * (1.0 / (D * KVH * HD))
        step.append(learning_rate * lax.rsqrt(mean + norm_eps))

    def update(pos, cc, k):
        rows = rows_of(pos, cc)
        fresh = (pfull[k, rows, :].astype(F32) - step[k] * gfull[k, rows, :].astype(F32)).astype(BF)
        newr[k, rows, :] = (mix_alpha * fresh.astype(F32) + (1.0 - mix_alpha) * rwv[k, rows, :].astype(F32)).astype(BF)
        return fresh

    def settle(pos, k):
        update(pos, c, k)
        g2.from_sib(pos, k)
        update(pos, 1 - c, k)

    for k in (f, g):
        newp[k] = update(OWN, c, k)
        g2.from_sib(OWN, k)
        update(OWN, 1 - c, k)
    for pos in (LFT, RGT, ZED):
        settle(pos, f)
    g2.take(ZOP, f)
    g2.take(ZLF, g)
    g2.take(ZRG, g)
    for pos in (LFT, RGT, ZED):
        settle(pos, g)
    settle(OPP, f)
    g2.take(ZOP, g)
    settle(OPP, g)
    for k in (f, g):
        settle(ZLF, k)
        settle(ZRG, k)
    settle(ZOP, f)
    settle(ZOP, g)

    g1.finish()
    g2.finish()
    all_sent(score_buf.at[pl.ds(0, NT - 1)], sc_send.at[0], sc_recv.at[0])
    all_sent(sq_tensor.at[pl.ds(0, NT - 1)], qt_send.at[0], qt_recv.at[0])
    all_sent(sq_shard.at[pl.ds(0, NS - 1)], qs_send.at[0], qs_recv.at[0])
    all_sent(sib_send, rs_sib_send.at[0], rs_sib_recv.at[0, 0])
    all_sent(stage.at[pl.ds(0, 7)], rs_send.at[0], rs_recv.at[0, 0])


def write_out(new_rows, new_reference, margin, rows_out, reference_out, margin_out, sem):
    copies = [
        pltpu.make_async_copy(new_reference, reference_out, sem.at[0]),
        pltpu.make_async_copy(new_rows, rows_out, sem.at[1]),
    ]
    for copy in copies:
        copy.start()
    margin_out[0] = margin[0, 0]
    for copy in copies:
        copy.wait()


def body(hidden_in, policy_weights, reference_weights, policy_queries, reference_queries, readout, lengths):
    rope, rope_t = rope_constants()
    anywhere = pl.BlockSpec(memory_space=pl.ANY)
    vmem = pl.BlockSpec(memory_space=pltpu.VMEM)
    dma = pltpu.SemaphoreType.DMA
    block = (2, ROWS, HD)
    new_rows, new_reference, margins = pl.pallas_call(
        kernel,
        out_shape=(
            pltpu.VMEM(block, BF),
            pltpu.VMEM((2, D, HD), BF),
            pltpu.VMEM((8, HD), F32),
        ),
        in_specs=[anywhere] * 6 + [pl.BlockSpec(memory_space=pltpu.SMEM)] + [anywhere] * 2,
        out_specs=(vmem, vmem, vmem),
        scratch_shapes=[
            pltpu.VMEM((TOK, D), BF),
            pltpu.VMEM((2, D, HD), BF),
            pltpu.VMEM((2, D, HD), BF),
            pltpu.VMEM((2, D, HD), BF),
            pltpu.VMEM((TOK, HEADS * HD), BF),
            pltpu.VMEM((TOK, HEADS * HD), BF),
            pltpu.VMEM((TOK, HEADS * HD), BF),
            pltpu.VMEM((2, LEN, HD), F32),
            pltpu.VMEM((2, HD // 2, LEN), F32),
            pltpu.VMEM((TOK, 2 * HD), F32),
            pltpu.VMEM((TOK, HD), BF),
            pltpu.VMEM((TOK, HD), BF),
            pltpu.VMEM((2 * HD, TOK), BF),
            pltpu.VMEM((2, NB, HEADS * QB, LEN), F32),
            pltpu.VMEM((2, HD, TOK), F32),
            pltpu.VMEM((8, *block), F32),
            pltpu.VMEM((8, *block), BF),
            pltpu.VMEM((8, *block), BF),
            pltpu.VMEM((8, *block), BF),
            pltpu.VMEM((7, *block), BF),
            pltpu.VMEM((NT, 8, HD), F32),
            pltpu.VMEM((NT, 2, 8, HD), F32),
            pltpu.VMEM((NS, 2, 8, HD), F32),
            dma((3,)), dma((7,)),
            dma((1,)), dma((8, 2)), dma((1,)), dma((8, 2)),
            dma((1,)), dma((8, 2)), dma((1,)), dma((8, 2)),
            dma((1,)), dma((8, 2)), dma((1,)), dma((7, 2)),
            dma((1,)), dma((1,)), dma((1,)), dma((1,)), dma((1,)), dma((1,)),
        ],
        compiler_params=pltpu.CompilerParams(
            collective_id=0, has_side_effects=True, vmem_limit_bytes=54 * 1024 * 1024
        ),
        cost_estimate=pl.CostEstimate(flops=12_000_000_000, bytes_accessed=24_000_000, transcendentals=2_000_000),
    )(
        hidden_in, policy_weights, reference_weights, policy_queries, reference_queries, readout, lengths,
        jnp.asarray(rope), jnp.asarray(rope_t),
    )
    return pl.pallas_call(
        write_out,
        out_shape=(
            jax.ShapeDtypeStruct(block, BF),
            jax.ShapeDtypeStruct((2, D, HD), BF),
            jax.ShapeDtypeStruct((1,), F32),
        ),
        in_specs=[vmem] * 3,
        out_specs=(anywhere, anywhere, pl.BlockSpec(memory_space=pltpu.SMEM)),
        scratch_shapes=[dma((2,))],
        compiler_params=pltpu.CompilerParams(vmem_limit_bytes=1024 * 1024),
    )(*(pltpu.with_memory_space_constraint(a, pltpu.VMEM) for a in (new_rows, new_reference, margins)))


def solution(mesh):
    return jax.shard_map(
        body,
        mesh=mesh,
        in_specs=(
            P("shard", None),
            P(None, "shard", "tensor"),
            P(None, None, "tensor"),
            P("shard", "tensor"),
            P("shard", "tensor"),
            P("shard", "tensor"),
            P("shard"),
        ),
        out_specs=(P(None, "shard", "tensor"), P(None, None, "tensor"), P("shard")),
        check_vma=False,
    )
```

```python
import math

import jax
import jax.numpy as jnp
import numpy as np
from jax import lax
from jax.experimental import pallas as pl
from jax.experimental.pallas import tpu as pltpu
from jax.sharding import PartitionSpec as P

D = 8192
HD = 128
KVH = 8
QH = 32
LEN = 384
TOK = 2 * LEN
HEADS = 4
NS = 16
NT = 8
ROWS = D // NS
QB = 128
NB = LEN // QB

rope_base = 1000000.0
dpo_beta = 0.1
learning_rate = 0.2
mix_alpha = 0.6
norm_eps = 1e-06

MESH = pl.DeviceIdType.MESH
BF = jnp.bfloat16
F32 = jnp.float32

OWN, LFT, RGT, ZED, OPP, ZLF, ZRG, ZOP = range(8)
PLACE = {"OWN": OWN, "L": LFT, "R": RGT, "Z": ZED, "O": OPP, "ZL": ZLF, "ZR": ZRG, "ZO": ZOP}
HALF = ROWS // 2

PLAN = (
    ("co", 0, 0), ("cs", 2, 0), ("key",), ("cs", 0, 0), ("cs", 5, 1), ("cs", 2, 1), ("co", 1, 1), ("cs", 1, 1),
    ("co", 5, 1), ("co", 6, 1), ("co", 2, 0), ("co", 0, 1), ("co", 2, 1), ("cs", 0, 1), ("put", 0, 1),
    ("x", "R1", 1), ("put", 0, 0), ("x", "R1", 0), ("put", 5, 3), ("x", "R5r", 3), ("put", 2, 1), ("x", "R2l", 1),
    ("co", 5, 0), ("put", 2, 2), ("x", "R2l", 2), ("put", 1, 2), ("x", "R2r", 2), ("put", 1, 3), ("co", 6, 0),
    ("cs", 4, 0), ("put", 2, 0), ("put", 2, 3), ("cs", 7, 0), ("x", "R2r", 3), ("x", "R2l", 3), ("cs", 1, 0),
    ("put", 0, 3), ("put", 0, 2), ("x", "R1", 2), ("co", 4, 1), ("co", 7, 1), ("cs", 3, 1), ("x", "R1", 3),
    ("cs", 6, 0), ("co", 3, 0), ("x", "R2l", 0), ("cs", 3, 0), ("cs", 4, 1), ("cs", 6, 1), ("co", 1, 0),
    ("put", 1, 0), ("x", "R2r", 0), ("put", 1, 1), ("co", 7, 0), ("x", "R2r", 1), ("cs", 7, 1), ("co", 3, 1),
    ("cs", 5, 0), ("put", 6, 0), ("co", 4, 0), ("put", 3, 1), ("x", "R3", 1), ("put", 3, 0), ("put", 4, 2),
    ("x", "R4", 2), ("x", "R5l", 0), ("put", 6, 2), ("put", 4, 3), ("x", "R4", 3), ("put", 3, 2), ("x", "R3", 2),
    ("put", 5, 1), ("x", "R3", 0), ("put", 4, 0), ("x", "R4", 0), ("put", 3, 3), ("x", "R3", 3), ("x", "R5r", 1),
    ("put", 4, 1), ("x", "R4", 1), ("put", 6, 1), ("x", "R5l", 1), ("x", "R5l", 2), ("put", 5, 2), ("x", "R5r", 2),
    ("put", 5, 0), ("x", "R5r", 0), ("put", 6, 3), ("x", "R5l", 3), ("put", 7, 1), ("x", "ownz", 1),
    ("x", "own+", 1), ("x", "own-", 1), ("put", 7, 2), ("x", "ownz", 2), ("x", "own+", 2), ("x", "own-", 2),
    ("put", 7, 0), ("x", "own+", 0), ("put", 7, 3), ("x", "ownz", 3), ("x", "own-", 3), ("qt",), ("x", "ownz", 0),
    ("x", "own+", 3), ("t", "R", 1), ("x", "fO", 1), ("t", "L", 1), ("t", "Z", 1), ("x", "z-", 1), ("t", "R", 2),
    ("t", "L", 2), ("x", "fO", 2), ("t", "Z", 2), ("t", "L", 0), ("x", "fO", 0), ("t", "R", 3), ("x", "fO", 3),
    ("qsum",), ("t", "Z", 3), ("x", "z+", 3), ("x", "z-", 3), ("t", "O", 1), ("x", "zz", 1), ("t", "L", 3),
    ("t", "Z", 0), ("x", "z+", 0), ("x", "z-", 0), ("t", "O", 2), ("x", "zz", 2), ("t", "ZR", 1), ("x", "z+", 1),
    ("x", "z-", 2), ("t", "O", 3), ("x", "zz", 3), ("t", "O", 0), ("x", "zz", 0), ("x", "z+", 2), ("x", "own-", 0),
    ("t", "ZL", 3), ("t", "ZR", 3), ("t", "ZO", 1), ("step",), ("u", "ZO", 1), ("u", "L", 0), ("u", "ZR", 3),
    ("us", "R", 3), ("us", "Z", 1), ("us", "ZR", 1), ("u", "O", 2), ("u", "O", 3), ("u", "OWN", 2),
    ("us", "OWN", 2), ("u", "OWN", 0), ("u", "R", 3), ("u", "Z", 0), ("u", "L", 1), ("t", "ZR", 0), ("us", "ZL", 3),
    ("u", "ZR", 0), ("us", "ZR", 3), ("us", "L", 2), ("us", "ZO", 1), ("us", "R", 1), ("us", "OWN", 0),
    ("us", "O", 3), ("u", "L", 3), ("u", "ZL", 3), ("u", "Z", 2), ("us", "O", 1), ("us", "Z", 0), ("u", "OWN", 3),
    ("u", "L", 2), ("us", "R", 2), ("u", "O", 0), ("us", "L", 1), ("u", "Z", 3), ("t", "ZL", 1), ("u", "ZL", 1),
    ("us", "ZR", 0), ("t", "ZR", 2), ("u", "ZR", 2), ("t", "ZL", 2), ("t", "R", 0), ("u", "R", 0), ("t", "ZO", 0),
    ("u", "ZL", 2), ("t", "ZL", 0), ("t", "ZO", 3), ("u", "ZO", 3), ("us", "OWN", 1), ("us", "O", 2),
    ("us", "Z", 2), ("t", "ZO", 2), ("u", "ZO", 2), ("us", "OWN", 3), ("u", "Z", 1), ("us", "Z", 3),
    ("us", "ZL", 1), ("us", "L", 0), ("u", "ZO", 0), ("us", "ZR", 2), ("u", "ZL", 0), ("us", "ZL", 2),
    ("u", "O", 1), ("us", "R", 0), ("u", "R", 1), ("us", "ZO", 0), ("us", "ZL", 0), ("us", "O", 0), ("us", "ZO", 3),
    ("u", "ZR", 1), ("u", "R", 2), ("u", "OWN", 1), ("us", "ZO", 2), ("us", "L", 3),
)


def rope_constants():
    positions = np.arange(LEN, dtype=np.float32)
    index = np.arange(HD // 2, dtype=np.float32)
    frequency = (np.float32(rope_base) ** (np.float32(-2.0) * index / np.float32(HD))).astype(np.float32)
    angles = (positions[:, None] * frequency[None, :]).astype(np.float32)
    cosine, sine = np.cos(angles), np.sin(angles)
    wide_cos = np.concatenate([cosine, cosine], axis=1)
    wide_sin = np.concatenate([-sine, sine], axis=1)
    return np.stack([wide_cos, wide_sin]), np.stack([wide_cos.T[: HD // 2], sine.T])


def dot(a, b, contract=((1,), (0,))):
    return lax.dot_general(a, b, (contract, ((), ())), preferred_element_type=F32)


def kernel(
    hid, pw, rw, pq, rq, ro, lens, rope, rope_t,
    newp, newr, marg,
    normed, pfull, gfull, rwv, pqv, rqv, rov, ropev, ropetv,
    acc, keys, values, cot, probs, grad_t,
    partial, sib_send, sib_recv, stage, net_recv,
    score_buf, sq_tensor, sq_shard,
    hid_sem, load_sem,
    g1_send, g1_recv, s1_send, s1_recv,
    g2_send, g2_recv, s2_send, s2_recv,
    rs_sib_send, rs_sib_recv, rs_send, rs_recv,
    sc_send, sc_recv, qt_send, qt_recv, qs_send, qs_recv,
):
    s = lax.axis_index("shard")
    t = lax.axis_index("tensor")
    x, h, c = s // 4, (s // 2) % 2, s % 2

    def shard_of(xx, hh, cc):
        return lax.rem(xx, 4) * 4 + hh * 2 + cc

    left = (shard_of(x + 3, h, c), t)
    right = (shard_of(x + 1, h, c), t)
    zed = (shard_of(x, 1 - h, c), t)
    sib = (shard_of(x, h, 1 - c), t)

    pair = {
        OWN: (x, h),
        LFT: (x + 3, h),
        RGT: (x + 1, h),
        ZED: (x, 1 - h),
        OPP: (x + 2, h),
        ZLF: (x + 3, 1 - h),
        ZRG: (x + 1, 1 - h),
        ZOP: (x + 2, 1 - h),
    }

    def rows_of(pos, cc):
        return pl.ds(pl.multiple_of(shard_of(*pair[pos], cc) * ROWS, ROWS), ROWS)

    def pair_rows(pos):
        return pl.ds(pl.multiple_of(shard_of(*pair[pos], 0) * ROWS, 2 * ROWS), 2 * ROWS)

    def send(src, dst, send_sem, recv_sem, device):
        pltpu.make_async_remote_copy(
            src_ref=src, dst_ref=dst, send_sem=send_sem, recv_sem=recv_sem,
            device_id=device, device_id_type=MESH,
        ).start()

    def all_sent(amount, send_sem, recv_sem):
        pltpu.make_async_remote_copy(
            src_ref=amount, dst_ref=amount, send_sem=send_sem, recv_sem=recv_sem,
            device_id=sib, device_id_type=MESH,
        ).wait_send()

    def arrived(dst, recv_sem, send_sem, device):
        pltpu.make_async_remote_copy(
            src_ref=dst, dst_ref=dst, send_sem=send_sem, recv_sem=recv_sem,
            device_id=device, device_id_type=MESH,
        ).wait_recv()

    barrier = pltpu.get_barrier_semaphore()
    for device in (left, right, zed, sib):
        pl.semaphore_signal(barrier, inc=1, device_id=device, device_id_type=MESH)
    for r in range(1, NT):
        pl.semaphore_signal(barrier, inc=1, device_id=(s, lax.rem(t + r, NT)), device_id_type=MESH)

    def load_hidden(b):
        copy = pltpu.make_async_copy(hid.at[pl.ds(256 * b, 256)], normed.at[pl.ds(256 * b, 256)], hid_sem.at[b])
        copy.start()
        return copy

    def load(src, dst, i):
        copy = pltpu.make_async_copy(src, dst, load_sem.at[i])
        copy.start()
        return copy

    hid_copies = [load_hidden(0)]
    pl.semaphore_wait(barrier, 4 + NT - 1)

    class Gather:
        def __init__(self, buf, own, lead, send_sem, recv_sem, sib_send_sem, sib_recv_sem):
            self.buf, self.own, self.lead = buf, own, lead
            self.send_sem, self.recv_sem = send_sem, recv_sem
            self.sib_send_sem, self.sib_recv_sem = sib_send_sem, sib_recv_sem

        def block(self, pos, cc, k):
            return self.buf.at[k, rows_of(pos, cc), :]

        def to(self, src, dst_pos_here, k, arrive_as, device):
            send(src, self.block(dst_pos_here, c, k), self.send_sem.at[0], self.recv_sem.at[arrive_as, k], device)

        def to_sib(self, src, pos, k):
            send(src, self.block(pos, c, k), self.sib_send_sem.at[0], self.sib_recv_sem.at[pos, k], sib)

        def start(self, k):
            src = self.own(k)
            self.to(src, OWN, k, LFT, right)
            self.to(src, OWN, k, RGT, left)
            self.to(src, OWN, k, ZED, zed)
            self.to_sib(src, OWN, k)

        def start_both(self):
            f, g = self.lead, 1 - self.lead
            self.to(self.own(f), OWN, f, LFT, right)
            self.to(self.own(g), OWN, g, RGT, left)
            self.to(self.own(f), OWN, f, ZED, zed)
            self.to(self.own(g), OWN, g, LFT, right)
            self.to(self.own(f), OWN, f, RGT, left)
            self.to(self.own(g), OWN, g, ZED, zed)
            self.to_sib(self.own(f), OWN, f)
            self.to_sib(self.own(g), OWN, g)

        def take(self, pos, k):
            lead = k == self.lead
            device = {LFT: left, RGT: right, ZED: zed, OPP: left if lead else right, ZLF: left, ZRG: right, ZOP: zed}[pos]
            arrived(self.block(pos, c, k), self.recv_sem.at[pos, k], self.send_sem.at[0], device)
            src = self.block(pos, c, k)
            if pos == LFT and lead:
                self.to(src, pos, k, OPP, right)
            if pos == RGT and not lead:
                self.to(src, pos, k, OPP, left)
            if pos == ZED:
                self.to(src, pos, k, ZLF, right)
                self.to(src, pos, k, ZRG, left)
            if pos == OPP:
                self.to(src, pos, k, ZOP, zed)
            self.to_sib(src, pos, k)

        def from_sib(self, pos, k):
            arrived(self.block(pos, 1 - c, k), self.sib_recv_sem.at[pos, k], self.sib_send_sem.at[0], sib)

        def finish(self):
            all_sent(self.buf.at[:, pl.ds(0, 7 * ROWS), :], self.send_sem.at[0], self.recv_sem.at[LFT, 0])
            all_sent(self.buf.at[:, pl.ds(0, 8 * ROWS), :], self.sib_send_sem.at[0], self.sib_recv_sem.at[OWN, 0])

    g1 = Gather(pfull, lambda k: pw.at[k], 0, g1_send, g1_recv, s1_send, s1_recv)
    g1.start_both()

    hid_copies += [load_hidden(1), load_hidden(2)]
    own_rows = rows_of(OWN, c)
    loads = [
        load(rw, rwv, 0),
        load(rq, rqv, 1),
        load(ro, rov, 2),
        load(rope, ropev, 3),
        load(pw, pfull.at[:, own_rows, :], 4),
        load(pq, pqv, 5),
        load(rope_t, ropetv, 6),
    ]

    def normalise(b):
        hid_copies[b].wait()

        @pl.loop(0, 8)
        def _(i):
            rows = pl.ds(pl.multiple_of(256 * b + i * 32, 32), 32)
            total = jnp.zeros((32, 512), F32)
            for j in range(D // 512):
                part = normed[rows, pl.ds(512 * j, 512)].astype(F32)
                total = total + part * part
            inverse = lax.rsqrt(jnp.sum(total, axis=-1, keepdims=True) * (1.0 / D) + norm_eps)
            for j in range(D // 512):
                cols = pl.ds(512 * j, 512)
                normed[rows, cols] = (normed[rows, cols].astype(F32) * inverse).astype(BF)

    def project(weights, cols, first):
        both = jnp.concatenate([weights[0, cols, :], weights[1, cols, :]], axis=1)
        product = dot(normed[:, cols], both)
        acc[...] = product if first else acc[...] + product

    def project_reference(first, last):
        if first == 0:
            project(rwv, pl.ds(0, 1024), True)
            first = 1

        @pl.loop(first, last)
        def _(j):
            project(rwv, pl.ds(pl.multiple_of(j * 1024, 1024), 1024), False)

    def heads_out():
        for q in range(2):
            rows = pl.ds(LEN * q, LEN)
            raw = acc[rows, 0:HD] * (D ** -0.5)
            turned = raw * ropev[0] + pltpu.roll(raw, HD // 2, 1) * ropev[1]
            keys[rows, :] = turned.astype(BF)
            values[rows, :] = (acc[rows, HD:] * (D ** -0.5)).astype(BF)

    def stacked(ref, q, b):
        rows = pl.ds(LEN * q + QB * b, QB)
        return jnp.concatenate([ref[rows, pl.ds(HD * g, HD)] for g in range(HEADS)], axis=0)

    def attend(q, b, queries, keep):
        n = QB * (b + 1)
        live = lens[q]
        seen = pl.ds(LEN * q, n)
        logits = dot(stacked(queries, q, b), keys[seen, :], ((1,), (1,))) * (math.log2(math.e) / math.sqrt(HD))
        key_at = lax.broadcasted_iota(jnp.int32, (1, n), 1)
        logits = logits + jnp.where(key_at < live, 0.0, -1e30)
        at = lax.broadcasted_iota(jnp.int32, (QB, QB), 0)
        after = lax.broadcasted_iota(jnp.int32, (QB, QB), 1) > at
        corner = jnp.where(after, -1e30, 0.0)
        corner = jnp.concatenate([corner] * HEADS, axis=0)
        if b == 0:
            logits = logits + corner
        else:
            logits = jnp.concatenate([logits[:, : n - QB], logits[:, n - QB :] + corner], axis=1)
        exponent = jnp.exp2(logits - jnp.max(logits, axis=-1, keepdims=True))
        probability = exponent * (1.0 / jnp.sum(exponent, axis=-1, keepdims=True))
        if keep:
            probs[q, b, :, 0:n] = probability
        attended = dot(probability.astype(BF), values[seen, :]).astype(BF).astype(F32)
        product = attended * stacked(rov, q, b).astype(F32)
        real = QB * b + lax.rem(lax.broadcasted_iota(jnp.int32, product.shape, 0), QB) < live
        product = jnp.where(real, product, 0.0)
        return jnp.sum(product.reshape(HEADS * QB // 8, 8, HD), axis=0)

    def scores(queries, keep):
        chosen = jnp.zeros((8, HD), F32)
        rejected = jnp.zeros((8, HD), F32)
        for b in range(NB):
            chosen = chosen + attend(0, b, queries, keep)
            rejected = rejected + attend(1, b, queries, keep)
        return chosen - rejected

    for b in range(3):
        normalise(b)
    for pos, k in ((LFT, 0), (RGT, 1), (ZED, 0)):
        g1.take(pos, k)
    loads[0].wait()
    project_reference(0, 5)
    for pos, k in ((ZED, 1), (LFT, 1), (RGT, 0)):
        g1.take(pos, k)
    project_reference(5, 8)
    for i in (1, 2, 3):
        loads[i].wait()
    heads_out()
    g1.take(OPP, 0)
    g1.take(OPP, 1)
    score_buf[t] = -scores(rqv, False)

    def project_policy(pos, first=False):
        for k in range(2):
            g1.from_sib(pos, k)
        project(pfull, pair_rows(pos), first)

    for i in (4, 5, 6):
        loads[i].wait()
    project_policy(OWN, True)
    g1.take(ZLF, 0)
    g1.take(ZRG, 0)
    for pos in (LFT, RGT, ZED):
        project_policy(pos)
    g1.take(ZOP, 0)
    g1.take(ZLF, 1)
    g1.take(ZRG, 1)
    project_policy(OPP)
    project_policy(ZLF)
    g1.take(ZOP, 1)
    project_policy(ZRG)
    project_policy(ZOP)

    heads_out()
    score_buf[t] = score_buf[t] + scores(pqv, True)
    for r in range(1, NT):
        send(score_buf.at[t], score_buf.at[t], sc_send.at[0], sc_recv.at[0], (s, lax.rem(t + r, NT)))

    def out_cotangent(q, b):
        out_cot = stacked(rov, q, b).astype(F32) * ((-1.0 if q == 0 else 1.0) / math.sqrt(QH * HD))
        real = QB * b + lax.rem(lax.broadcasted_iota(jnp.int32, out_cot.shape, 0), QB) < lens[q]
        return jnp.where(real, out_cot, 0.0).astype(BF)

    def pull_value(q, b):
        n = QB * (b + 1)
        seen = pl.ds(LEN * q, n)
        value_t = dot(out_cotangent(q, b), probs[q, b, :, 0:n].astype(BF), ((0,), (0,)))
        if b == NB - 1:
            grad_t[1, :, seen] = value_t
        else:
            grad_t[1, :, seen] += value_t

    def pull_key(q, b):
        n = QB * (b + 1)
        seen = pl.ds(LEN * q, n)
        probability = probs[q, b, :, 0:n]
        prob_cot = dot(out_cotangent(q, b), values[seen, :], ((1,), (1,))).astype(BF).astype(F32)
        weighted = probability * prob_cot
        logit_cot = weighted - probability * jnp.sum(weighted, axis=-1, keepdims=True)
        key_t = dot(stacked(pqv, q, b), logit_cot.astype(BF), ((0,), (0,)))
        if b == NB - 1:
            grad_t[0, :, seen] = key_t
        else:
            grad_t[0, :, seen] += key_t

    def value_cotangent():
        for q in range(2):
            for b in reversed(range(NB)):
                pull_value(q, b)
        cot[HD:, :] = grad_t[1].astype(BF)

    def key_cotangent(q):
        for b in reversed(range(NB)):
            pull_key(q, b)
        tokens = pl.ds(LEN * q, LEN)
        key_grad = (grad_t[0, :, tokens] * (1.0 / math.sqrt(HD))).astype(BF).astype(F32)
        upper, lower = key_grad[: HD // 2], key_grad[HD // 2 :]
        cosine, sine = ropetv[0], ropetv[1]
        cot[0 : HD // 2, tokens] = (upper * cosine + lower * sine).astype(BF)
        cot[HD // 2 : HD, tokens] = (lower * cosine - upper * sine).astype(BF)

    value_cotangent()
    key_cotangent(0)

    arrived(score_buf.at[pl.ds(0, NT - 1)], sc_recv.at[0], sc_send.at[0], (s, lax.rem(t + 1, NT)))
    score_total = score_buf[0]
    for r in range(1, NT):
        score_total = score_total + score_buf[r]
    score_total = jnp.sum(jnp.sum(score_total, axis=1, keepdims=True), axis=0, keepdims=True)
    margin = score_total * (dpo_beta / math.sqrt(QH * HD))
    marg[...] = jnp.broadcast_to(margin, (8, HD))
    weight = 1.0 / (1.0 + jnp.exp(margin))

    def product_of(pos, cc, k):
        out = dot(cot[pl.ds(HD * k, HD), :], normed[:, rows_of(pos, cc)]) * weight
        return out.T

    order = (ZOP, ZRG, ZLF, OPP, ZED, RGT, LFT, OWN)
    SLOT_Z1, SLOT_R2L, SLOT_R2R, SLOT_3, SLOT_Z4, SLOT_5L, SLOT_5R = range(7)

    def kind(q):
        return 1 - q // 2

    def turns_right(q):
        return q % 2 == 0

    def part(q):
        return pl.ds(HALF * (q % 2), HALF)

    def piece(pos, cc, q):
        return pl.ds(pl.multiple_of(shard_of(*pair[pos], cc) * ROWS + HALF * (q % 2), HALF), HALF)

    def grad_piece(pos, cc, q):
        return gfull.at[kind(q), piece(pos, cc, q), :]

    def push(i, q, slot, device):
        src, dst = stage.at[i, kind(q), part(q)], net_recv.at[slot, kind(q), part(q)]
        send(src, dst, rs_send.at[0], rs_recv.at[slot, q], device)

    def pull_net(slot, q, device):
        arrived(net_recv.at[slot, kind(q), part(q)], rs_recv.at[slot, q], rs_send.at[0], device)
        return net_recv[slot, kind(q), part(q)].astype(F32)

    def spread(pos, q, arrive_as, device):
        send(grad_piece(pos, c, q), grad_piece(pos, c, q), g2_send.at[0], g2_recv.at[arrive_as, q], device)

    def spread_sib(pos, q):
        send(grad_piece(pos, c, q), grad_piece(pos, c, q), s2_send.at[0], s2_recv.at[pos, q], sib)

    def compute_sib(i, k):
        sib_send[i, k] = product_of(order[i], 1 - c, k).astype(BF)
        send(sib_send.at[i, k], sib_recv.at[i, k], rs_sib_send.at[0], rs_sib_recv.at[i, k], sib)

    def compute_own(i, k):
        partial[i, k] = product_of(order[i], c, k)

    def start(name, q):
        if name == "R1":
            push(0, q, SLOT_Z1, zed)
        elif name == "R2r":
            push(1, q, SLOT_R2L, right)
        elif name == "R2l":
            push(2, q, SLOT_R2R, left)
        elif name == "R3":
            push(3, q, SLOT_3, right if turns_right(q) else left)
        elif name == "R4":
            push(4, q, SLOT_Z4, zed)
        elif name == "R5r":
            push(5, q, SLOT_5L, right)
        elif name == "R5l":
            push(6, q, SLOT_5R, left)
        elif name == "own+":
            spread(OWN, q, LFT, right)
        elif name == "own-":
            spread(OWN, q, RGT, left)
        elif name == "ownz":
            spread(OWN, q, ZED, zed)
        elif name == "fO" and turns_right(q):
            spread(LFT, q, OPP, right)
        elif name == "fO":
            spread(RGT, q, OPP, left)
        elif name == "zz":
            spread(OPP, q, ZOP, zed)
        elif name == "z+":
            spread(ZED, q, ZLF, right)
        elif name == "z-":
            spread(ZED, q, ZRG, left)
        else:
            raise ValueError(name)

    from_core = set()
    summed = set()

    def put(i, q):
        k = kind(q)
        if (i, k) not in from_core:
            from_core.add((i, k))
            arrived(sib_recv.at[i, k], rs_sib_recv.at[i, k], rs_sib_send.at[0], sib)
        total = partial[i, k, part(q)] + sib_recv[i, k, part(q)].astype(F32)
        if i == 3:
            total = total + pull_net(SLOT_Z1, q, zed)
        elif i == 4:
            total = total + pull_net(SLOT_R2L, q, left) + pull_net(SLOT_R2R, q, right)
        elif i == 5 and turns_right(q):
            total = total + pull_net(SLOT_3, q, left)
        elif i == 6 and not turns_right(q):
            total = total + pull_net(SLOT_3, q, right)
        if i < 7:
            stage[i, k, part(q)] = total.astype(BF)
            return
        total = total + pull_net(SLOT_Z4, q, zed)
        total = total + pull_net(SLOT_5L, q, left)
        total = total + pull_net(SLOT_5R, q, right)
        gfull[k, piece(OWN, c, q), :] = total.astype(BF)
        spread_sib(OWN, q)
        squares = jnp.sum((total * total).reshape(HALF // 8, 8, HD), axis=0)
        sq_tensor[t, k] = sq_tensor[t, k] + squares if k in summed else squares
        summed.add(k)

    def take(pos, q):
        device = {
            LFT: left, RGT: right, ZED: zed, OPP: left if turns_right(q) else right, ZLF: left, ZRG: right, ZOP: zed,
        }[pos]
        arrived(grad_piece(pos, c, q), g2_recv.at[pos, q], g2_send.at[0], device)
        spread_sib(pos, q)

    def send_squares():
        for r in range(1, NT):
            send(sq_tensor.at[t], sq_tensor.at[t], qt_send.at[0], qt_recv.at[0], (s, lax.rem(t + r, NT)))

    def add_squares():
        arrived(sq_tensor.at[pl.ds(0, NT - 1)], qt_recv.at[0], qt_send.at[0], (s, lax.rem(t + 1, NT)))
        squares = sq_tensor[0]
        for r in range(1, NT):
            squares = squares + sq_tensor[r]
        sq_shard[s] = squares
        for r in range(1, NS):
            send(sq_shard.at[s], sq_shard.at[s], qs_send.at[0], qs_recv.at[0], (lax.rem(s + r, NS), t))

    step = []

    def find_step():
        arrived(sq_shard.at[pl.ds(0, NS - 1)], qs_recv.at[0], qs_send.at[0], (lax.rem(s + 1, NS), t))
        squares = sq_shard[0]
        for r in range(1, NS):
            squares = squares + sq_shard[r]
        for k in range(2):
            mean = jnp.sum(jnp.sum(squares[k], axis=1, keepdims=True), axis=0, keepdims=True) * (1.0 / (D * KVH * HD))
            step.append(learning_rate * lax.rsqrt(mean + norm_eps))

    def update(pos, cc, q):
        k, rows = kind(q), piece(pos, cc, q)
        fresh = (pfull[k, rows, :].astype(F32) - step[k] * gfull[k, rows, :].astype(F32)).astype(BF)
        newr[k, rows, :] = (mix_alpha * fresh.astype(F32) + (1.0 - mix_alpha) * rwv[k, rows, :].astype(F32)).astype(BF)
        return fresh

    def update_own_core(pos, q):
        fresh = update(pos, c, q)
        if pos == OWN:
            newp[kind(q), part(q), :] = fresh

    def update_other_core(pos, q):
        arrived(grad_piece(pos, 1 - c, q), s2_recv.at[pos, q], s2_send.at[0], sib)
        update(pos, 1 - c, q)

    act = {
        "key": lambda: key_cotangent(1),
        "cs": lambda i, first: compute_sib(i, 1 - first),
        "co": lambda i, first: compute_own(i, 1 - first),
        "put": put,
        "x": start,
        "t": lambda pos, q: take(PLACE[pos], q),
        "qt": send_squares,
        "qsum": add_squares,
        "step": find_step,
        "u": lambda pos, q: update_own_core(PLACE[pos], q),
        "us": lambda pos, q: update_other_core(PLACE[pos], q),
    }
    for name, *rest in PLAN:
        act[name](*rest)

    g1.finish()
    all_sent(gfull.at[:, pl.ds(0, 7 * ROWS), :], g2_send.at[0], g2_recv.at[LFT, 0])
    all_sent(gfull.at[:, pl.ds(0, 8 * ROWS), :], s2_send.at[0], s2_recv.at[OWN, 0])
    all_sent(score_buf.at[pl.ds(0, NT - 1)], sc_send.at[0], sc_recv.at[0])
    all_sent(sq_tensor.at[pl.ds(0, NT - 1)], qt_send.at[0], qt_recv.at[0])
    all_sent(sq_shard.at[pl.ds(0, NS - 1)], qs_send.at[0], qs_recv.at[0])
    all_sent(sib_send, rs_sib_send.at[0], rs_sib_recv.at[0, 0])
    all_sent(stage.at[pl.ds(0, 7)], rs_send.at[0], rs_recv.at[0, 0])


def write_out(new_rows, new_reference, margin, rows_out, reference_out, margin_out, sem):
    copies = [
        pltpu.make_async_copy(new_reference, reference_out, sem.at[0]),
        pltpu.make_async_copy(new_rows, rows_out, sem.at[1]),
    ]
    for copy in copies:
        copy.start()
    margin_out[0] = margin[0, 0]
    for copy in copies:
        copy.wait()


def body(hidden_in, policy_weights, reference_weights, policy_queries, reference_queries, readout, lengths):
    rope, rope_t = rope_constants()
    anywhere = pl.BlockSpec(memory_space=pl.ANY)
    vmem = pl.BlockSpec(memory_space=pltpu.VMEM)
    dma = pltpu.SemaphoreType.DMA
    block = (2, ROWS, HD)
    new_rows, new_reference, margins = pl.pallas_call(
        kernel,
        out_shape=(
            pltpu.VMEM(block, BF),
            pltpu.VMEM((2, D, HD), BF),
            pltpu.VMEM((8, HD), F32),
        ),
        in_specs=[anywhere] * 6 + [pl.BlockSpec(memory_space=pltpu.SMEM)] + [anywhere] * 2,
        out_specs=(vmem, vmem, vmem),
        scratch_shapes=[
            pltpu.VMEM((TOK, D), BF),
            pltpu.VMEM((2, D, HD), BF),
            pltpu.VMEM((2, D, HD), BF),
            pltpu.VMEM((2, D, HD), BF),
            pltpu.VMEM((TOK, HEADS * HD), BF),
            pltpu.VMEM((TOK, HEADS * HD), BF),
            pltpu.VMEM((TOK, HEADS * HD), BF),
            pltpu.VMEM((2, LEN, HD), F32),
            pltpu.VMEM((2, HD // 2, LEN), F32),
            pltpu.VMEM((TOK, 2 * HD), F32),
            pltpu.VMEM((TOK, HD), BF),
            pltpu.VMEM((TOK, HD), BF),
            pltpu.VMEM((2 * HD, TOK), BF),
            pltpu.VMEM((2, NB, HEADS * QB, LEN), F32),
            pltpu.VMEM((2, HD, TOK), F32),
            pltpu.VMEM((8, *block), F32),
            pltpu.VMEM((8, *block), BF),
            pltpu.VMEM((8, *block), BF),
            pltpu.VMEM((8, *block), BF),
            pltpu.VMEM((7, *block), BF),
            pltpu.VMEM((NT, 8, HD), F32),
            pltpu.VMEM((NT, 2, 8, HD), F32),
            pltpu.VMEM((NS, 2, 8, HD), F32),
            dma((3,)), dma((7,)),
            dma((1,)), dma((8, 2)), dma((1,)), dma((8, 2)),
            dma((1,)), dma((8, 4)), dma((1,)), dma((8, 4)),
            dma((1,)), dma((8, 2)), dma((1,)), dma((7, 4)),
            dma((1,)), dma((1,)), dma((1,)), dma((1,)), dma((1,)), dma((1,)),
        ],
        compiler_params=pltpu.CompilerParams(
            collective_id=0, has_side_effects=True, vmem_limit_bytes=54 * 1024 * 1024
        ),
        cost_estimate=pl.CostEstimate(flops=12_000_000_000, bytes_accessed=24_000_000, transcendentals=2_000_000),
    )(
        hidden_in, policy_weights, reference_weights, policy_queries, reference_queries, readout, lengths,
        jnp.asarray(rope), jnp.asarray(rope_t),
    )
    return pl.pallas_call(
        write_out,
        out_shape=(
            jax.ShapeDtypeStruct(block, BF),
            jax.ShapeDtypeStruct((2, D, HD), BF),
            jax.ShapeDtypeStruct((1,), F32),
        ),
        in_specs=[vmem] * 3,
        out_specs=(anywhere, anywhere, pl.BlockSpec(memory_space=pltpu.SMEM)),
        scratch_shapes=[dma((2,))],
        compiler_params=pltpu.CompilerParams(vmem_limit_bytes=1024 * 1024),
    )(*(pltpu.with_memory_space_constraint(a, pltpu.VMEM) for a in (new_rows, new_reference, margins)))


def solution(mesh):
    return jax.shard_map(
        body,
        mesh=mesh,
        in_specs=(
            P("shard", None),
            P(None, "shard", "tensor"),
            P(None, None, "tensor"),
            P("shard", "tensor"),
            P("shard", "tensor"),
            P("shard", "tensor"),
            P("shard"),
        ),
        out_specs=(P(None, "shard", "tensor"), P(None, None, "tensor"), P("shard")),
        check_vma=False,
    )
```

```python
import math

import jax
import jax.numpy as jnp
import numpy as np
from jax import lax
from jax.experimental import pallas as pl
from jax.experimental.pallas import tpu as pltpu
from jax.sharding import PartitionSpec as P

D = 8192
HD = 128
KVH = 8
QH = 32
LEN = 384
TOK = 2 * LEN
HEADS = 4
NS = 16
NT = 8
ROWS = D // NS
QB = 128
NB = LEN // QB

rope_base = 1000000.0
dpo_beta = 0.1
learning_rate = 0.2
mix_alpha = 0.6
norm_eps = 1e-06

MESH = pl.DeviceIdType.MESH
BF = jnp.bfloat16
F32 = jnp.float32

OWN, LFT, RGT, ZED, OPP, ZLF, ZRG, ZOP = range(8)
PLACE = {"OWN": OWN, "L": LFT, "R": RGT, "Z": ZED, "O": OPP, "ZL": ZLF, "ZR": ZRG, "ZO": ZOP}
HALF = ROWS // 2

PLAN = (
    ("cs", 0, 0), ("co", 0, 0), ("cs", 2, 0), ("cs", 1, 0), ("co", 1, 0), ("co", 2, 0), ("key",), ("cs", 1, 1),
    ("cs", 0, 1), ("put", 0, 0), ("x", "R1", 0), ("put", 1, 1), ("x", "R2r", 1), ("put", 1, 0), ("x", "R2r", 0),
    ("put", 2, 0), ("x", "R2l", 0), ("co", 0, 1), ("put", 2, 1), ("x", "R2l", 1), ("cs", 2, 1), ("cs", 5, 1),
    ("cs", 3, 1), ("put", 0, 1), ("x", "R1", 1), ("co", 3, 1), ("cs", 4, 0), ("put", 0, 3), ("x", "R1", 3),
    ("co", 5, 0), ("co", 2, 1), ("cs", 3, 0), ("co", 1, 1), ("put", 1, 3), ("x", "R2r", 3), ("put", 2, 2),
    ("x", "R2l", 2), ("put", 2, 3), ("x", "R2l", 3), ("put", 0, 2), ("x", "R1", 2), ("put", 1, 2), ("x", "R2r", 2),
    ("co", 6, 0), ("co", 5, 1), ("co", 7, 1), ("cs", 6, 0), ("co", 6, 1), ("co", 7, 0), ("co", 3, 0), ("put", 3, 0),
    ("x", "R3", 0), ("cs", 6, 1), ("co", 4, 0), ("put", 4, 1), ("x", "R4", 1), ("put", 3, 1), ("x", "R3", 1),
    ("put", 4, 0), ("x", "R4", 0), ("co", 4, 1), ("put", 5, 3), ("x", "R5r", 3), ("cs", 5, 0), ("put", 6, 0),
    ("cs", 4, 1), ("cs", 7, 0), ("put", 3, 3), ("x", "R3", 3), ("cs", 7, 1), ("x", "R5l", 0), ("put", 6, 2),
    ("put", 3, 2), ("x", "R3", 2), ("put", 5, 1), ("x", "R5r", 1), ("put", 4, 3), ("x", "R4", 3), ("put", 4, 2),
    ("x", "R4", 2), ("put", 5, 0), ("put", 6, 1), ("x", "R5l", 1), ("x", "R5r", 0), ("put", 6, 3), ("x", "R5l", 3),
    ("x", "R5l", 2), ("put", 5, 2), ("x", "R5r", 2), ("put", 7, 1), ("x", "ownz", 1), ("x", "own+", 1),
    ("x", "own-", 1), ("put", 7, 0), ("x", "ownz", 0), ("x", "own+", 0), ("put", 7, 3), ("x", "own-", 3),
    ("x", "ownz", 3), ("x", "own-", 0), ("put", 7, 2), ("x", "own+", 2), ("x", "ownz", 2), ("qt",), ("t", "L", 1),
    ("t", "R", 1), ("x", "fO", 1), ("t", "Z", 1), ("x", "z+", 1), ("t", "L", 0), ("x", "fO", 0), ("t", "R", 3),
    ("x", "fO", 3), ("t", "Z", 0), ("t", "L", 2), ("x", "fO", 2), ("t", "R", 0), ("t", "Z", 3), ("x", "z-", 3),
    ("qsum",), ("x", "z-", 1), ("t", "ZL", 1), ("t", "O", 1), ("x", "zz", 1), ("t", "Z", 2), ("x", "z+", 2),
    ("x", "z+", 3), ("x", "own-", 2), ("t", "O", 0), ("x", "zz", 0), ("t", "O", 3), ("x", "z+", 0), ("x", "z-", 0),
    ("t", "O", 2), ("x", "zz", 2), ("t", "ZR", 3), ("x", "zz", 3), ("x", "own+", 3), ("x", "z-", 2), ("t", "ZL", 2),
    ("t", "ZR", 1), ("t", "ZO", 1), ("step",), ("us", "Z", 0), ("u", "OWN", 0), ("u", "L", 0), ("us", "ZR", 3),
    ("us", "Z", 2), ("u", "R", 0), ("u", "Z", 3), ("u", "R", 1), ("t", "R", 2), ("u", "O", 3), ("u", "R", 2),
    ("u", "Z", 0), ("us", "L", 2), ("us", "ZL", 2), ("us", "R", 0), ("us", "ZR", 1), ("u", "OWN", 3),
    ("t", "ZL", 3), ("u", "R", 3), ("us", "O", 0), ("u", "ZR", 3), ("t", "ZL", 0), ("t", "ZR", 0), ("u", "ZR", 0),
    ("u", "ZL", 0), ("us", "L", 1), ("us", "Z", 3), ("u", "Z", 2), ("us", "R", 2), ("us", "ZO", 1), ("t", "ZO", 2),
    ("u", "ZO", 2), ("u", "ZL", 1), ("t", "ZO", 0), ("t", "L", 3), ("u", "ZO", 0), ("us", "ZL", 3), ("t", "ZO", 3),
    ("t", "ZR", 2), ("us", "ZL", 0), ("u", "ZO", 3), ("us", "ZR", 0), ("u", "ZR", 2), ("u", "ZO", 1),
    ("us", "ZL", 1), ("u", "L", 2), ("u", "ZL", 3), ("us", "OWN", 0), ("u", "OWN", 2), ("us", "ZO", 2),
    ("us", "O", 2), ("u", "O", 2), ("us", "L", 0), ("us", "ZO", 0), ("us", "L", 3), ("us", "R", 3), ("u", "ZR", 1),
    ("u", "ZL", 2), ("u", "O", 0), ("us", "ZR", 2), ("us", "O", 1), ("us", "ZO", 3), ("u", "Z", 1), ("us", "R", 1),
    ("u", "O", 1), ("u", "OWN", 1), ("us", "OWN", 1), ("u", "L", 1), ("us", "OWN", 2), ("u", "L", 3),
    ("us", "O", 3), ("us", "OWN", 3), ("us", "Z", 1),
)


def rope_constants():
    positions = np.arange(LEN, dtype=np.float32)
    index = np.arange(HD // 2, dtype=np.float32)
    frequency = (np.float32(rope_base) ** (np.float32(-2.0) * index / np.float32(HD))).astype(np.float32)
    angles = (positions[:, None] * frequency[None, :]).astype(np.float32)
    cosine, sine = np.cos(angles), np.sin(angles)
    wide_cos = np.concatenate([cosine, cosine], axis=1)
    wide_sin = np.concatenate([-sine, sine], axis=1)
    return np.stack([wide_cos, wide_sin]), np.stack([wide_cos.T[: HD // 2], sine.T])


def dot(a, b, contract=((1,), (0,))):
    return lax.dot_general(a, b, (contract, ((), ())), preferred_element_type=F32)


def kernel(
    hid, pw, rw, pq, rq, ro, lens, rope, rope_t,
    newp, newr, marg,
    normed, pfull, gfull, rwv, pqv, rqv, rov, ropev, ropetv,
    acc, keys, values, cot, probs, grad_t,
    partial, sib_send, sib_recv, stage, net_recv,
    score_buf, sq_tensor, sq_shard,
    hid_sem, load_sem,
    g1_send, g1_recv, s1_send, s1_recv,
    g2_send, g2_recv, s2_send, s2_recv,
    rs_sib_send, rs_sib_recv, rs_send, rs_recv,
    sc_send, sc_recv, qt_send, qt_recv, qs_send, qs_recv,
):
    s = lax.axis_index("shard")
    t = lax.axis_index("tensor")
    x, h, c = s // 4, (s // 2) % 2, s % 2

    def shard_of(xx, hh, cc):
        return lax.rem(xx, 4) * 4 + hh * 2 + cc

    left = (shard_of(x + 3, h, c), t)
    right = (shard_of(x + 1, h, c), t)
    zed = (shard_of(x, 1 - h, c), t)
    sib = (shard_of(x, h, 1 - c), t)

    pair = {
        OWN: (x, h),
        LFT: (x + 3, h),
        RGT: (x + 1, h),
        ZED: (x, 1 - h),
        OPP: (x + 2, h),
        ZLF: (x + 3, 1 - h),
        ZRG: (x + 1, 1 - h),
        ZOP: (x + 2, 1 - h),
    }

    def rows_of(pos, cc):
        return pl.ds(pl.multiple_of(shard_of(*pair[pos], cc) * ROWS, ROWS), ROWS)

    def pair_rows(pos):
        return pl.ds(pl.multiple_of(shard_of(*pair[pos], 0) * ROWS, 2 * ROWS), 2 * ROWS)

    def send(src, dst, send_sem, recv_sem, device):
        pltpu.make_async_remote_copy(
            src_ref=src, dst_ref=dst, send_sem=send_sem, recv_sem=recv_sem,
            device_id=device, device_id_type=MESH,
        ).start()

    def all_sent(amount, send_sem, recv_sem):
        pltpu.make_async_remote_copy(
            src_ref=amount, dst_ref=amount, send_sem=send_sem, recv_sem=recv_sem,
            device_id=sib, device_id_type=MESH,
        ).wait_send()

    def arrived(dst, recv_sem, send_sem, device):
        pltpu.make_async_remote_copy(
            src_ref=dst, dst_ref=dst, send_sem=send_sem, recv_sem=recv_sem,
            device_id=device, device_id_type=MESH,
        ).wait_recv()

    barrier = pltpu.get_barrier_semaphore()
    for device in (left, right, zed, sib):
        pl.semaphore_signal(barrier, inc=1, device_id=device, device_id_type=MESH)
    for r in range(1, NT):
        pl.semaphore_signal(barrier, inc=1, device_id=(s, lax.rem(t + r, NT)), device_id_type=MESH)

    def load_hidden(b):
        copy = pltpu.make_async_copy(hid.at[pl.ds(256 * b, 256)], normed.at[pl.ds(256 * b, 256)], hid_sem.at[b])
        copy.start()
        return copy

    def load(src, dst, i):
        copy = pltpu.make_async_copy(src, dst, load_sem.at[i])
        copy.start()
        return copy

    hid_copies = [load_hidden(0)]
    pl.semaphore_wait(barrier, 4 + NT - 1)

    class Gather:
        def __init__(self, buf, own, lead, send_sem, recv_sem, sib_send_sem, sib_recv_sem):
            self.buf, self.own, self.lead = buf, own, lead
            self.send_sem, self.recv_sem = send_sem, recv_sem
            self.sib_send_sem, self.sib_recv_sem = sib_send_sem, sib_recv_sem

        def block(self, pos, cc, k):
            return self.buf.at[k, rows_of(pos, cc), :]

        def to(self, src, dst_pos_here, k, arrive_as, device):
            send(src, self.block(dst_pos_here, c, k), self.send_sem.at[0], self.recv_sem.at[arrive_as, k], device)

        def to_sib(self, src, pos, k):
            send(src, self.block(pos, c, k), self.sib_send_sem.at[0], self.sib_recv_sem.at[pos, k], sib)

        def start(self, k):
            src = self.own(k)
            self.to(src, OWN, k, LFT, right)
            self.to(src, OWN, k, RGT, left)
            self.to(src, OWN, k, ZED, zed)
            self.to_sib(src, OWN, k)

        def start_both(self):
            f, g = self.lead, 1 - self.lead
            self.to(self.own(f), OWN, f, LFT, right)
            self.to(self.own(g), OWN, g, RGT, left)
            self.to(self.own(f), OWN, f, ZED, zed)
            self.to(self.own(g), OWN, g, LFT, right)
            self.to(self.own(f), OWN, f, RGT, left)
            self.to(self.own(g), OWN, g, ZED, zed)
            self.to_sib(self.own(f), OWN, f)
            self.to_sib(self.own(g), OWN, g)

        def take(self, pos, k):
            lead = k == self.lead
            device = {LFT: left, RGT: right, ZED: zed, OPP: left if lead else right, ZLF: left, ZRG: right, ZOP: zed}[pos]
            arrived(self.block(pos, c, k), self.recv_sem.at[pos, k], self.send_sem.at[0], device)
            src = self.block(pos, c, k)
            if pos == LFT and lead:
                self.to(src, pos, k, OPP, right)
            if pos == RGT and not lead:
                self.to(src, pos, k, OPP, left)
            if pos == ZED:
                self.to(src, pos, k, ZLF, right)
                self.to(src, pos, k, ZRG, left)
            if pos == OPP:
                self.to(src, pos, k, ZOP, zed)
            self.to_sib(src, pos, k)

        def from_sib(self, pos, k):
            arrived(self.block(pos, 1 - c, k), self.sib_recv_sem.at[pos, k], self.sib_send_sem.at[0], sib)

        def finish(self):
            all_sent(self.buf.at[:, pl.ds(0, 7 * ROWS), :], self.send_sem.at[0], self.recv_sem.at[LFT, 0])
            all_sent(self.buf.at[:, pl.ds(0, 8 * ROWS), :], self.sib_send_sem.at[0], self.sib_recv_sem.at[OWN, 0])

    g1 = Gather(pfull, lambda k: pw.at[k], 0, g1_send, g1_recv, s1_send, s1_recv)
    g1.start_both()

    hid_copies += [load_hidden(1), load_hidden(2)]
    own_rows = rows_of(OWN, c)
    loads = [
        load(rw, rwv, 0),
        load(rq, rqv, 1),
        load(ro, rov, 2),
        load(rope, ropev, 3),
        load(pw, pfull.at[:, own_rows, :], 4),
        load(pq, pqv, 5),
        load(rope_t, ropetv, 6),
    ]

    def normalise(b):
        hid_copies[b].wait()

        @pl.loop(0, 8)
        def _(i):
            rows = pl.ds(pl.multiple_of(256 * b + i * 32, 32), 32)
            total = jnp.zeros((32, 512), F32)
            for j in range(D // 512):
                part = normed[rows, pl.ds(512 * j, 512)].astype(F32)
                total = total + part * part
            inverse = lax.rsqrt(jnp.sum(total, axis=-1, keepdims=True) * (1.0 / D) + norm_eps)
            for j in range(D // 512):
                cols = pl.ds(512 * j, 512)
                normed[rows, cols] = (normed[rows, cols].astype(F32) * inverse).astype(BF)

    def project(weights, cols, first):
        both = jnp.concatenate([weights[0, cols, :], weights[1, cols, :]], axis=1)
        product = dot(normed[:, cols], both)
        acc[...] = product if first else acc[...] + product

    def project_reference(first, last):
        if first == 0:
            project(rwv, pl.ds(0, 1024), True)
            first = 1

        @pl.loop(first, last)
        def _(j):
            project(rwv, pl.ds(pl.multiple_of(j * 1024, 1024), 1024), False)

    def heads_out():
        for q in range(2):
            rows = pl.ds(LEN * q, LEN)
            raw = acc[rows, 0:HD] * (D ** -0.5)
            turned = raw * ropev[0] + pltpu.roll(raw, HD // 2, 1) * ropev[1]
            keys[rows, :] = turned.astype(BF)
            values[rows, :] = (acc[rows, HD:] * (D ** -0.5)).astype(BF)

    def stacked(ref, q, b):
        rows = pl.ds(LEN * q + QB * b, QB)
        return jnp.concatenate([ref[rows, pl.ds(HD * g, HD)] for g in range(HEADS)], axis=0)

    def attend(q, b, queries, keep):
        n = QB * (b + 1)
        live = lens[q]
        seen = pl.ds(LEN * q, n)
        logits = dot(stacked(queries, q, b), keys[seen, :], ((1,), (1,))) * (math.log2(math.e) / math.sqrt(HD))
        key_at = lax.broadcasted_iota(jnp.int32, (1, n), 1)
        logits = logits + jnp.where(key_at < live, 0.0, -1e30)
        at = lax.broadcasted_iota(jnp.int32, (QB, QB), 0)
        after = lax.broadcasted_iota(jnp.int32, (QB, QB), 1) > at
        corner = jnp.where(after, -1e30, 0.0)
        corner = jnp.concatenate([corner] * HEADS, axis=0)
        if b == 0:
            logits = logits + corner
        else:
            logits = jnp.concatenate([logits[:, : n - QB], logits[:, n - QB :] + corner], axis=1)
        exponent = jnp.exp2(logits - jnp.max(logits, axis=-1, keepdims=True))
        probability = exponent * (1.0 / jnp.sum(exponent, axis=-1, keepdims=True))
        if keep:
            probs[q, b, :, 0:n] = probability
        attended = dot(probability.astype(BF), values[seen, :]).astype(BF).astype(F32)
        product = attended * stacked(rov, q, b).astype(F32)
        real = QB * b + lax.rem(lax.broadcasted_iota(jnp.int32, product.shape, 0), QB) < live
        product = jnp.where(real, product, 0.0)
        return jnp.sum(product.reshape(HEADS * QB // 8, 8, HD), axis=0)

    def scores(queries, keep):
        chosen = jnp.zeros((8, HD), F32)
        rejected = jnp.zeros((8, HD), F32)
        for b in range(NB):
            chosen = chosen + attend(0, b, queries, keep)
            rejected = rejected + attend(1, b, queries, keep)
        return chosen - rejected

    normalise(0)
    normalise(1)
    for pos, k in ((LFT, 0), (RGT, 1), (ZED, 0)):
        g1.take(pos, k)
    normalise(2)
    loads[0].wait()
    project_reference(0, 3)
    for pos, k in ((ZED, 1), (LFT, 1), (RGT, 0)):
        g1.take(pos, k)
    project_reference(3, 8)
    g1.take(OPP, 0)
    g1.take(OPP, 1)
    for i in (1, 2, 3):
        loads[i].wait()
    heads_out()
    score_buf[t] = -scores(rqv, False)

    def project_policy(pos, first=False):
        for k in range(2):
            g1.from_sib(pos, k)
        project(pfull, pair_rows(pos), first)

    for i in (4, 5, 6):
        loads[i].wait()
    project_policy(OWN, True)
    g1.take(ZLF, 0)
    g1.take(ZRG, 0)
    for pos in (LFT, RGT, ZED):
        project_policy(pos)
    g1.take(ZOP, 0)
    g1.take(ZLF, 1)
    g1.take(ZRG, 1)
    project_policy(OPP)
    project_policy(ZLF)
    g1.take(ZOP, 1)
    project_policy(ZRG)
    project_policy(ZOP)

    heads_out()
    score_buf[t] = score_buf[t] + scores(pqv, True)
    for r in range(1, NT):
        send(score_buf.at[t], score_buf.at[t], sc_send.at[0], sc_recv.at[0], (s, lax.rem(t + r, NT)))

    def out_cotangent(q, b):
        out_cot = stacked(rov, q, b).astype(F32) * ((-1.0 if q == 0 else 1.0) / math.sqrt(QH * HD))
        real = QB * b + lax.rem(lax.broadcasted_iota(jnp.int32, out_cot.shape, 0), QB) < lens[q]
        return jnp.where(real, out_cot, 0.0).astype(BF)

    def pull_value(q, b):
        n = QB * (b + 1)
        seen = pl.ds(LEN * q, n)
        value_t = dot(out_cotangent(q, b), probs[q, b, :, 0:n].astype(BF), ((0,), (0,)))
        if b == NB - 1:
            grad_t[1, :, seen] = value_t
        else:
            grad_t[1, :, seen] += value_t

    def pull_key(q, b):
        n = QB * (b + 1)
        seen = pl.ds(LEN * q, n)
        probability = probs[q, b, :, 0:n]
        prob_cot = dot(out_cotangent(q, b), values[seen, :], ((1,), (1,))).astype(BF).astype(F32)
        weighted = probability * prob_cot
        logit_cot = weighted - probability * jnp.sum(weighted, axis=-1, keepdims=True)
        key_t = dot(stacked(pqv, q, b), logit_cot.astype(BF), ((0,), (0,)))
        if b == NB - 1:
            grad_t[0, :, seen] = key_t
        else:
            grad_t[0, :, seen] += key_t

    def value_cotangent():
        for q in range(2):
            for b in reversed(range(NB)):
                pull_value(q, b)
        cot[HD:, :] = grad_t[1].astype(BF)

    def key_cotangent(q):
        for b in reversed(range(NB)):
            pull_key(q, b)
        tokens = pl.ds(LEN * q, LEN)
        key_grad = (grad_t[0, :, tokens] * (1.0 / math.sqrt(HD))).astype(BF).astype(F32)
        upper, lower = key_grad[: HD // 2], key_grad[HD // 2 :]
        cosine, sine = ropetv[0], ropetv[1]
        cot[0 : HD // 2, tokens] = (upper * cosine + lower * sine).astype(BF)
        cot[HD // 2 : HD, tokens] = (lower * cosine - upper * sine).astype(BF)

    value_cotangent()
    key_cotangent(0)

    order = (ZOP, ZRG, ZLF, OPP, ZED, RGT, LFT, OWN)

    def product_of(pos, cc, k):
        return dot(cot[pl.ds(HD * k, HD), :], normed[:, rows_of(pos, cc)]).T

    for i in range(2):
        acc[0:ROWS, pl.ds(HD * i, HD)] = product_of(order[i], 1 - c, 1)
    last = product_of(order[2], 1 - c, 1)
    acc[ROWS:, 0:HD] = last[:HALF]
    acc[ROWS:, HD:] = last[HALF:]
    partial[0, 1] = product_of(order[0], c, 1)

    def ready_product(i):
        if i < 2:
            return acc[0:ROWS, pl.ds(HD * i, HD)]
        return jnp.concatenate([acc[ROWS:, 0:HD], acc[ROWS:, HD:]], axis=0)

    arrived(score_buf.at[pl.ds(0, NT - 1)], sc_recv.at[0], sc_send.at[0], (s, lax.rem(t + 1, NT)))
    score_total = score_buf[0]
    for r in range(1, NT):
        score_total = score_total + score_buf[r]
    score_total = jnp.sum(jnp.sum(score_total, axis=1, keepdims=True), axis=0, keepdims=True)
    margin = score_total * (dpo_beta / math.sqrt(QH * HD))
    marg[...] = jnp.broadcast_to(margin, (8, HD))
    weight = 1.0 / (1.0 + jnp.exp(margin))

    SLOT_Z1, SLOT_R2L, SLOT_R2R, SLOT_3, SLOT_Z4, SLOT_5L, SLOT_5R = range(7)

    def kind(q):
        return 1 - q // 2

    def turns_right(q):
        return q % 2 == 0

    def part(q):
        return pl.ds(HALF * (q % 2), HALF)

    def piece(pos, cc, q):
        return pl.ds(pl.multiple_of(shard_of(*pair[pos], cc) * ROWS + HALF * (q % 2), HALF), HALF)

    def grad_piece(pos, cc, q):
        return gfull.at[kind(q), piece(pos, cc, q), :]

    def push(i, q, slot, device):
        src, dst = stage.at[i, kind(q), part(q)], net_recv.at[slot, kind(q), part(q)]
        send(src, dst, rs_send.at[0], rs_recv.at[slot, q], device)

    def pull_net(slot, q, device):
        arrived(net_recv.at[slot, kind(q), part(q)], rs_recv.at[slot, q], rs_send.at[0], device)
        return net_recv[slot, kind(q), part(q)].astype(F32)

    def spread(pos, q, arrive_as, device):
        send(grad_piece(pos, c, q), grad_piece(pos, c, q), g2_send.at[0], g2_recv.at[arrive_as, q], device)

    def spread_sib(pos, q):
        send(grad_piece(pos, c, q), grad_piece(pos, c, q), s2_send.at[0], s2_recv.at[pos, q], sib)

    def compute_sib(i, k):
        product = ready_product(i) if i < 3 and k == 1 else product_of(order[i], 1 - c, k)
        sib_send[i, k] = (product * weight).astype(BF)
        send(sib_send.at[i, k], sib_recv.at[i, k], rs_sib_send.at[0], rs_sib_recv.at[i, k], sib)

    def compute_own(i, k):
        if (i, k) == (0, 1):
            return
        partial[i, k] = product_of(order[i], c, k)

    def start(name, q):
        if name == "R1":
            push(0, q, SLOT_Z1, zed)
        elif name == "R2r":
            push(1, q, SLOT_R2L, right)
        elif name == "R2l":
            push(2, q, SLOT_R2R, left)
        elif name == "R3":
            push(3, q, SLOT_3, right if turns_right(q) else left)
        elif name == "R4":
            push(4, q, SLOT_Z4, zed)
        elif name == "R5r":
            push(5, q, SLOT_5L, right)
        elif name == "R5l":
            push(6, q, SLOT_5R, left)
        elif name == "own+":
            spread(OWN, q, LFT, right)
        elif name == "own-":
            spread(OWN, q, RGT, left)
        elif name == "ownz":
            spread(OWN, q, ZED, zed)
        elif name == "fO" and turns_right(q):
            spread(LFT, q, OPP, right)
        elif name == "fO":
            spread(RGT, q, OPP, left)
        elif name == "zz":
            spread(OPP, q, ZOP, zed)
        elif name == "z+":
            spread(ZED, q, ZLF, right)
        elif name == "z-":
            spread(ZED, q, ZRG, left)
        else:
            raise ValueError(name)

    from_core = set()
    summed = set()

    def put(i, q):
        k = kind(q)
        if (i, k) not in from_core:
            from_core.add((i, k))
            arrived(sib_recv.at[i, k], rs_sib_recv.at[i, k], rs_sib_send.at[0], sib)
        total = partial[i, k, part(q)] * weight + sib_recv[i, k, part(q)].astype(F32)
        if i == 3:
            total = total + pull_net(SLOT_Z1, q, zed)
        elif i == 4:
            total = total + pull_net(SLOT_R2L, q, left) + pull_net(SLOT_R2R, q, right)
        elif i == 5 and turns_right(q):
            total = total + pull_net(SLOT_3, q, left)
        elif i == 6 and not turns_right(q):
            total = total + pull_net(SLOT_3, q, right)
        if i < 7:
            stage[i, k, part(q)] = total.astype(BF)
            return
        total = total + pull_net(SLOT_Z4, q, zed)
        total = total + pull_net(SLOT_5L, q, left)
        total = total + pull_net(SLOT_5R, q, right)
        gfull[k, piece(OWN, c, q), :] = total.astype(BF)
        spread_sib(OWN, q)
        squares = jnp.sum((total * total).reshape(HALF // 8, 8, HD), axis=0)
        sq_tensor[t, k] = sq_tensor[t, k] + squares if k in summed else squares
        summed.add(k)

    def take(pos, q):
        device = {
            LFT: left, RGT: right, ZED: zed, OPP: left if turns_right(q) else right, ZLF: left, ZRG: right, ZOP: zed,
        }[pos]
        arrived(grad_piece(pos, c, q), g2_recv.at[pos, q], g2_send.at[0], device)
        spread_sib(pos, q)

    def send_squares():
        for r in range(1, NT):
            send(sq_tensor.at[t], sq_tensor.at[t], qt_send.at[0], qt_recv.at[0], (s, lax.rem(t + r, NT)))

    def add_squares():
        arrived(sq_tensor.at[pl.ds(0, NT - 1)], qt_recv.at[0], qt_send.at[0], (s, lax.rem(t + 1, NT)))
        squares = sq_tensor[0]
        for r in range(1, NT):
            squares = squares + sq_tensor[r]
        sq_shard[s] = squares
        for r in range(1, NS):
            send(sq_shard.at[s], sq_shard.at[s], qs_send.at[0], qs_recv.at[0], (lax.rem(s + r, NS), t))

    step = []

    def find_step():
        arrived(sq_shard.at[pl.ds(0, NS - 1)], qs_recv.at[0], qs_send.at[0], (lax.rem(s + 1, NS), t))
        squares = sq_shard[0]
        for r in range(1, NS):
            squares = squares + sq_shard[r]
        for k in range(2):
            mean = jnp.sum(jnp.sum(squares[k], axis=1, keepdims=True), axis=0, keepdims=True) * (1.0 / (D * KVH * HD))
            step.append(learning_rate * lax.rsqrt(mean + norm_eps))

    def update(pos, cc, q):
        k, rows = kind(q), piece(pos, cc, q)
        fresh = (pfull[k, rows, :].astype(F32) - step[k] * gfull[k, rows, :].astype(F32)).astype(BF)
        newr[k, rows, :] = (mix_alpha * fresh.astype(F32) + (1.0 - mix_alpha) * rwv[k, rows, :].astype(F32)).astype(BF)
        return fresh

    def update_own_core(pos, q):
        fresh = update(pos, c, q)
        if pos == OWN:
            newp[kind(q), part(q), :] = fresh

    def update_other_core(pos, q):
        arrived(grad_piece(pos, 1 - c, q), s2_recv.at[pos, q], s2_send.at[0], sib)
        update(pos, 1 - c, q)

    act = {
        "key": lambda: key_cotangent(1),
        "cs": lambda i, first: compute_sib(i, 1 - first),
        "co": lambda i, first: compute_own(i, 1 - first),
        "put": put,
        "x": start,
        "t": lambda pos, q: take(PLACE[pos], q),
        "qt": send_squares,
        "qsum": add_squares,
        "step": find_step,
        "u": lambda pos, q: update_own_core(PLACE[pos], q),
        "us": lambda pos, q: update_other_core(PLACE[pos], q),
    }
    for name, *rest in PLAN:
        act[name](*rest)

    g1.finish()
    all_sent(gfull.at[:, pl.ds(0, 7 * ROWS), :], g2_send.at[0], g2_recv.at[LFT, 0])
    all_sent(gfull.at[:, pl.ds(0, 8 * ROWS), :], s2_send.at[0], s2_recv.at[OWN, 0])
    all_sent(score_buf.at[pl.ds(0, NT - 1)], sc_send.at[0], sc_recv.at[0])
    all_sent(sq_tensor.at[pl.ds(0, NT - 1)], qt_send.at[0], qt_recv.at[0])
    all_sent(sq_shard.at[pl.ds(0, NS - 1)], qs_send.at[0], qs_recv.at[0])
    all_sent(sib_send, rs_sib_send.at[0], rs_sib_recv.at[0, 0])
    all_sent(stage.at[pl.ds(0, 7)], rs_send.at[0], rs_recv.at[0, 0])


def write_out(new_rows, new_reference, margin, rows_out, reference_out, margin_out, sem):
    copies = [
        pltpu.make_async_copy(new_reference, reference_out, sem.at[0]),
        pltpu.make_async_copy(new_rows, rows_out, sem.at[1]),
    ]
    for copy in copies:
        copy.start()
    margin_out[0] = margin[0, 0]
    for copy in copies:
        copy.wait()


def body(hidden_in, policy_weights, reference_weights, policy_queries, reference_queries, readout, lengths):
    rope, rope_t = rope_constants()
    anywhere = pl.BlockSpec(memory_space=pl.ANY)
    vmem = pl.BlockSpec(memory_space=pltpu.VMEM)
    dma = pltpu.SemaphoreType.DMA
    block = (2, ROWS, HD)
    new_rows, new_reference, margins = pl.pallas_call(
        kernel,
        out_shape=(
            pltpu.VMEM(block, BF),
            pltpu.VMEM((2, D, HD), BF),
            pltpu.VMEM((8, HD), F32),
        ),
        in_specs=[anywhere] * 6 + [pl.BlockSpec(memory_space=pltpu.SMEM)] + [anywhere] * 2,
        out_specs=(vmem, vmem, vmem),
        scratch_shapes=[
            pltpu.VMEM((TOK, D), BF),
            pltpu.VMEM((2, D, HD), BF),
            pltpu.VMEM((2, D, HD), BF),
            pltpu.VMEM((2, D, HD), BF),
            pltpu.VMEM((TOK, HEADS * HD), BF),
            pltpu.VMEM((TOK, HEADS * HD), BF),
            pltpu.VMEM((TOK, HEADS * HD), BF),
            pltpu.VMEM((2, LEN, HD), F32),
            pltpu.VMEM((2, HD // 2, LEN), F32),
            pltpu.VMEM((TOK, 2 * HD), F32),
            pltpu.VMEM((TOK, HD), BF),
            pltpu.VMEM((TOK, HD), BF),
            pltpu.VMEM((2 * HD, TOK), BF),
            pltpu.VMEM((2, NB, HEADS * QB, LEN), F32),
            pltpu.VMEM((2, HD, TOK), F32),
            pltpu.VMEM((8, *block), F32),
            pltpu.VMEM((8, *block), BF),
            pltpu.VMEM((8, *block), BF),
            pltpu.VMEM((8, *block), BF),
            pltpu.VMEM((7, *block), BF),
            pltpu.VMEM((NT, 8, HD), F32),
            pltpu.VMEM((NT, 2, 8, HD), F32),
            pltpu.VMEM((NS, 2, 8, HD), F32),
            dma((3,)), dma((7,)),
            dma((1,)), dma((8, 2)), dma((1,)), dma((8, 2)),
            dma((1,)), dma((8, 4)), dma((1,)), dma((8, 4)),
            dma((1,)), dma((8, 2)), dma((1,)), dma((7, 4)),
            dma((1,)), dma((1,)), dma((1,)), dma((1,)), dma((1,)), dma((1,)),
        ],
        compiler_params=pltpu.CompilerParams(
            collective_id=0, has_side_effects=True, vmem_limit_bytes=54 * 1024 * 1024
        ),
        cost_estimate=pl.CostEstimate(flops=12_000_000_000, bytes_accessed=24_000_000, transcendentals=2_000_000),
    )(
        hidden_in, policy_weights, reference_weights, policy_queries, reference_queries, readout, lengths,
        jnp.asarray(rope), jnp.asarray(rope_t),
    )
    return pl.pallas_call(
        write_out,
        out_shape=(
            jax.ShapeDtypeStruct(block, BF),
            jax.ShapeDtypeStruct((2, D, HD), BF),
            jax.ShapeDtypeStruct((1,), F32),
        ),
        in_specs=[vmem] * 3,
        out_specs=(anywhere, anywhere, pl.BlockSpec(memory_space=pltpu.SMEM)),
        scratch_shapes=[dma((2,))],
        compiler_params=pltpu.CompilerParams(vmem_limit_bytes=1024 * 1024),
    )(*(pltpu.with_memory_space_constraint(a, pltpu.VMEM) for a in (new_rows, new_reference, margins)))


def solution(mesh):
    return jax.shard_map(
        body,
        mesh=mesh,
        in_specs=(
            P("shard", None),
            P(None, "shard", "tensor"),
            P(None, None, "tensor"),
            P("shard", "tensor"),
            P("shard", "tensor"),
            P("shard", "tensor"),
            P("shard"),
        ),
        out_specs=(P(None, "shard", "tensor"), P(None, None, "tensor"), P("shard")),
        check_vma=False,
    )
```
